128 devices in a mesh: section: 2 (over x_lo), lat: 16 (over z, y), lon: 4 (over x_hi, core).
Axes of the slice: x: 4 (x_hi: 2, x_lo: 2; x = x_hi * 2 + x_lo), y: 4, z: 4, core: 2. Of those that a mesh axis runs over, the one named last changes fastest.
Arguments:
- state: bfloat16 [2, 112, 360, 1024], P('section', 'lat', 'lon'), may hold values from -6 to 6
- fresh: bfloat16 [112, 360, 1024], P('lat', 'lon'), may hold values from -6 to 6
- cutoff: int32 [3], replicated, may hold values from 0 to 15
- plan: int32 [2, 2], replicated, may hold values from 0 to 1
- lmax: int32 [2], replicated, may hold values from 56 to 112, as said below
- mmax: int32 [2], replicated, may hold values from 24 to 96, as said below
- cutoff_table: float32 [16, 1024], replicated, may hold values from -3 to 3
- norm_gains: float32 [2, 2, 2, 1024], P('section'), may hold values from 0.1 to 1.9
- filters: float32 [2, 2, 2, 112, 1024], P('section', None, None, None, 'lon'), may hold values from -5 to 5
- w_in: bfloat16 [2, 2, 1024, 4096], P('section', None, 'lat'), may hold values from -0.1875 to 0.1875
- w_out: bfloat16 [2, 2, 1024, 4096], P('section', None, 'lat'), may hold values from -0.09375 to 0.09375
Outputs:
- first_pass: bfloat16 [2, 112, 360, 1024], P('section', 'lat', 'lon')
- second_pass: bfloat16 [2, 112, 360, 1024], P('section', 'lat', 'lon')
The draws below stay inside these ranges and needn't reach their ends.
Inputs may be any that keep to these rules, and one draw needn't show every extreme that they name: `lmax`: some section keeps all 112 degrees in every draw. `mmax`: some section keeps all 96 wavenumbers in every draw.
All inputs are finite; a program needn't handle non-finite values.
Results may differ from the reference program's by a relative error of at most 0.01.
Values may be sent and summed in bfloat16 or wider, within the bound.
A program may use at most 384 MiB of HBM per device.

```python
import math
import jax
import jax.numpy as jnp
from jax import lax

D = 1024
FF = 4096
NLAT = 112
NLON = 360
MM = 96
LL = 112
NB = 2
NCUT = 16
SECTIONS = 2


def draw_bounded(key, lowest, highest):
    values = jax.random.randint(jax.random.fold_in(key, 11), (SECTIONS,), lowest, highest + 1)
    where_top = jax.random.randint(jax.random.fold_in(key, 23), (), 0, SECTIONS)
    return jnp.where(jnp.arange(SECTIONS) == where_top, highest, values).astype(jnp.int32)


def draw_lmax(key, part):
    return draw_bounded(jax.random.fold_in(key, 101), LL // 2, LL)


def draw_mmax(key, part):
    return draw_bounded(jax.random.fold_in(key, 202), MM // 4, MM)


def touch_ends(result, own_key, low, top_value):
    longest = result.shape.index(max(result.shape))
    spots = []
    for shift in (0, 1):
        where = [jax.random.randint(jax.random.fold_in(own_key, axis), (), 0, length) for axis, length in enumerate(result.shape)]
        where[longest] = (where[longest] + shift) % result.shape[longest]
        spots.append(tuple(where))
    return result.at[spots[0]].set(low).at[spots[1]].set(top_value)


def steps_of(stream_key, extent, shards, least, top_value):
    def one(position, blocks):
        heights = jax.random.uniform(jax.random.fold_in(jax.random.fold_in(stream_key, 6), position), (blocks,), jnp.float32, least / len(shards), top_value / len(shards))
        return jnp.repeat(jnp.exp(heights), extent[position] // blocks).reshape((-1,) + (1,) * (len(extent) - position - 1))

    loudness = one(*shards[0])
    for cut in shards[1:]:
        loudness = loudness * one(*cut)
    return loudness


def normal_values(stream_key, extent, deviation, reach, split=(), kind=jnp.bfloat16):
    entries = deviation * jax.random.normal(stream_key, extent, jnp.float32)
    if split:
        entries = entries * steps_of(stream_key, extent, split, -0.22, 0.18)
    return jnp.clip(entries, -reach, reach).astype(kind)


def setup_inputs(seed: int = 0) -> dict:
    arg_keys = jax.random.split(jax.random.key(seed), 12)
    state = normal_values(arg_keys[0], (SECTIONS, NLAT, NLON, D), 1.0, 6.0, ((0, 2), (1, 16), (2, 4)))
    fresh = normal_values(arg_keys[1], (NLAT, NLON, D), 1.0, 6.0, ((0, 16), (1, 4)))
    cutoff = jax.random.randint(arg_keys[2], (SECTIONS + 1,), 0, NCUT).astype(jnp.int32)
    plan = touch_ends(jax.random.randint(arg_keys[3], (2, SECTIONS), 0, NB), jax.random.fold_in(arg_keys[3], 1), 0, NB - 1).astype(jnp.int32)
    lmax = draw_lmax(jax.random.fold_in(arg_keys[11], 71), 0)
    mmax = draw_mmax(jax.random.fold_in(arg_keys[11], 71), 0)
    cutoff_table = normal_values(arg_keys[6], (NCUT, D), 0.5, 3.0, (), jnp.float32)
    norm_gains = jnp.clip(1.0 + 0.18 * jax.random.normal(arg_keys[7], (SECTIONS, NB, 2, D), jnp.float32), 0.1, 1.9)
    filters = normal_values(arg_keys[8], (SECTIONS, NB, 2, LL, D), 1.0, 5.0, ((0, 2), (4, 4)), jnp.float32)
    w_in = normal_values(arg_keys[9], (SECTIONS, NB, D, FF), D ** -0.5, 0.1875, ((0, 2), (2, 16)))
    w_out = normal_values(arg_keys[10], (SECTIONS, NB, D, FF), FF ** -0.5, 0.09375, ((0, 2), (2, 16)))
    return {"state": state, "fresh": fresh, "cutoff": cutoff, "plan": plan, "lmax": lmax, "mmax": mmax, "cutoff_table": cutoff_table, "norm_gains": norm_gains, "filters": filters, "w_in": w_in, "w_out": w_out}


def legendre_table(orders):
    rows = jnp.arange(NLAT, dtype=jnp.float32)
    theta = math.pi * (rows + 0.5) / NLAT
    cosine = jnp.cos(theta)
    sine = jnp.sin(theta)
    order = orders[:, None]
    log_start = 0.5 * jnp.log((2.0 * order + 1.0) / (4.0 * math.pi)) + jax.scipy.special.gammaln(order + 0.5) - jax.scipy.special.gammaln(0.5) - jax.scipy.special.gammaln(order + 1.0) + order * jnp.log(sine)[None, :]
    start = jnp.exp(log_start)

    def advance(carry, degree):
        last, before = carry
        level = degree.astype(jnp.float32)
        coef_a = jnp.sqrt(jnp.maximum(4.0 * level * level - 1.0, 1.0) / jnp.maximum(level * level - order * order, 1.0))
        coef_b = jnp.sqrt(jnp.maximum((level - 1.0) ** 2 - order * order, 0.0) / jnp.maximum(4.0 * (level - 1.0) ** 2 - 1.0, 1.0))
        general = coef_a * (cosine[None, :] * last - coef_b * before)
        fresh_row = jnp.where(level < order, jnp.zeros_like(start), jnp.where(level == order, start, general))
        return ((fresh_row, last), fresh_row)
    _, table = lax.scan(advance, (jnp.zeros_like(start), jnp.zeros_like(start)), jnp.arange(LL, dtype=jnp.int32))
    return table

def quadrature():
    rows = jnp.arange(NLAT, dtype=jnp.float32)
    theta = math.pi * (rows + 0.5) / NLAT
    return 2.0 * math.pi * (math.pi / NLAT) * jnp.sin(theta)

def fourier_tables(n_lon):
    columns = jnp.arange(n_lon, dtype=jnp.int32)
    orders = jnp.arange(MM, dtype=jnp.int32)
    phase = 2.0 * math.pi * (columns[:, None] * orders[None, :] % n_lon).astype(jnp.float32) / n_lon
    cos_fwd = jnp.cos(phase) / n_lon
    sin_fwd = -jnp.sin(phase) / n_lon
    weight = jnp.where(orders == 0, 1.0, 2.0).astype(jnp.float32)[:, None]
    inverse = jnp.stack([weight * jnp.cos(phase).T, -weight * jnp.sin(phase).T], 0)
    return (cos_fwd, sin_fwd, inverse)

def layer_norm(values, gain):
    center = values - lax.optimization_barrier(jnp.mean(values, axis=-1, keepdims=True))
    spread = lax.optimization_barrier(jnp.mean(center * center, axis=-1, keepdims=True))
    return center * lax.rsqrt(spread + 1e-05) * gain

def run_block(tokens, cut, gains, filt, weight_in, weight_out, l_max, m_max, cutoff_table, tables):
    plain, weighted, cos_fwd, sin_fwd, inverse = tables
    highest = lax.Precision.HIGHEST
    onehot = (jnp.arange(NCUT, dtype=jnp.int32) == cut).astype(jnp.float32)
    embed = jnp.dot(onehot, cutoff_table, precision=highest)
    base = tokens.astype(jnp.float32) + embed
    normed = layer_norm(base, gains[0]).astype(jnp.bfloat16)
    wide = normed.astype(jnp.float32)
    real_part = jnp.einsum('jkc,km->jmc', wide, cos_fwd, precision=highest)
    imag_part = jnp.einsum('jkc,km->jmc', wide, sin_fwd, precision=highest)
    spectrum = jnp.stack([real_part, imag_part], 1).astype(jnp.bfloat16)
    coeff = jnp.einsum('lmj,jrmc->rlmc', weighted, spectrum.astype(jnp.float32), precision=highest)
    keep = ((jnp.arange(LL, dtype=jnp.int32) < l_max)[:, None] & (jnp.arange(MM, dtype=jnp.int32) < m_max)[None, :]).astype(jnp.float32)[:, :, None]
    filt_re = filt[0][:, None, :]
    filt_im = filt[1][:, None, :]
    out_re = keep * (coeff[0] * filt_re - coeff[1] * filt_im)
    out_im = keep * (coeff[0] * filt_im + coeff[1] * filt_re)
    synthesis = jnp.einsum('lmj,rlmc->jrmc', plain, jnp.stack([out_re, out_im], 0), precision=highest).astype(jnp.bfloat16)
    spectral = jnp.einsum('jrmc,rmk->jkc', synthesis.astype(jnp.float32), inverse, precision=highest).astype(jnp.bfloat16)
    mixed = base + spectral.astype(jnp.float32)
    normed_two = layer_norm(mixed, gains[1]).astype(jnp.bfloat16)
    flat = normed_two.reshape(-1, normed_two.shape[-1])
    hidden = jax.nn.gelu(jnp.dot(flat, weight_in, preferred_element_type=jnp.float32)).astype(jnp.bfloat16)
    projected = lax.dot_general(hidden, weight_out, (((1,), (1,)), ((), ())), preferred_element_type=jnp.float32)
    return (mixed + projected.reshape(mixed.shape)).astype(jnp.bfloat16)

def reference(state, fresh, cutoff, plan, lmax, mmax, cutoff_table, norm_gains, filters, w_in, w_out):
    plain = legendre_table(jnp.arange(MM, dtype=jnp.float32))
    weighted = plain * quadrature()[None, None, :]
    cos_fwd, sin_fwd, inverse = fourier_tables(NLON)
    tables = (plain, weighted, cos_fwd, sin_fwd, inverse)

    def apply(tokens, section_num, tick):
        block_num = plan[tick, section_num]
        cut = cutoff[tick - section_num + SECTIONS - 1]
        gains = lax.dynamic_index_in_dim(norm_gains[section_num], block_num, 0, keepdims=False)
        filt = lax.dynamic_index_in_dim(filters[section_num], block_num, 0, keepdims=False)
        weight_in = lax.dynamic_index_in_dim(w_in[section_num], block_num, 0, keepdims=False)
        weight_out = lax.dynamic_index_in_dim(w_out[section_num], block_num, 0, keepdims=False)
        return run_block(tokens, cut, gains, filt, weight_in, weight_out, lmax[section_num], mmax[section_num], cutoff_table, tables)
    first = [apply(state[section_num], section_num, 0) for section_num in range(SECTIONS)]
    second = []
    for section_num in range(SECTIONS):
        incoming = fresh if section_num == 0 else first[section_num - 1]
        second.append(apply(incoming, section_num, 1))
    return (jnp.stack(first, 0), jnp.stack(second, 0))
```

```python
import math

import jax
import jax.numpy as jnp
import numpy as np
from jax import lax
from jax.sharding import PartitionSpec as P

MM = 96


def passed_along(value, axis, steps):
    count = lax.axis_size(axis)
    leading, last = (max(0, -steps), min(count, count - steps))
    return lax.ppermute(value, axis, [(source, source + steps) for source in range(leading, last)])


def legendre_table(n_orders, n_rows, n_degrees):
    theta = math.pi * (np.arange(n_rows) + 0.5) / n_rows
    cosine, sine = np.cos(theta), np.sin(theta)
    table = np.zeros((n_degrees, n_orders, n_rows))
    for m in range(n_orders):
        log_start = (
            0.5 * math.log((2.0 * m + 1.0) / (4.0 * math.pi))
            + math.lgamma(m + 0.5) - math.lgamma(0.5) - math.lgamma(m + 1.0)
        )
        table[m, m] = np.exp(log_start + m * np.log(sine))
        for l in range(m + 1, n_degrees):
            coef_a = math.sqrt((4.0 * l * l - 1.0) / (l * l - m * m))
            coef_b = math.sqrt(max((l - 1.0) ** 2 - m * m, 0.0) / max(4.0 * (l - 1.0) ** 2 - 1.0, 1.0))
            before = table[l - 2, m] if l - 2 >= m else 0.0
            table[l, m] = coef_a * (cosine * table[l - 1, m] - coef_b * before)
    quad = 2.0 * math.pi * (math.pi / n_rows) * sine
    return table, table * quad


def fourier_tables(n_lon):
    phase = 2.0 * math.pi * ((np.arange(n_lon)[:, None] * np.arange(MM)[None, :]) % n_lon) / n_lon
    weight = np.where(np.arange(MM) == 0, 1.0, 2.0)[:, None]
    inverse = np.stack([weight * np.cos(phase).T, -weight * np.sin(phase).T], 0)
    return (np.cos(phase) / n_lon, -np.sin(phase) / n_lon, inverse)


def layer_norm(values, gain):
    center = values - jnp.mean(values, axis=-1, keepdims=True)
    spread = jnp.mean(center * center, axis=-1, keepdims=True)
    return center * lax.rsqrt(spread + 1e-05) * gain


def pick(stack, index):
    return lax.dynamic_index_in_dim(stack, index, 0, keepdims=False)


def local(state, fresh, cutoff, plan, lmax, mmax, cutoff_table, norm_gains, filters, w_in, w_out):
    highest = lax.Precision.HIGHEST
    section_idx = lax.axis_index("section")
    lat_idx = lax.axis_index("lat")
    n_section = lax.axis_size("section")
    n_lat = lax.axis_size("lat")
    n_lon = lax.axis_size("lon")
    n_rows, n_cols, width = fresh.shape
    n_degrees = filters.shape[3]
    all_rows = n_rows * n_lat
    all_cols = n_cols * n_lon
    m_local = MM // n_lat
    m_global = lat_idx * m_local + jnp.arange(m_local, dtype=jnp.int32)
    tables = np.stack(legendre_table(MM, all_rows, n_degrees))
    tables = tables.reshape(2, n_degrees, n_lat, m_local, all_rows).transpose(2, 0, 1, 3, 4)
    plain, weighted = pick(jnp.asarray(tables.astype(jnp.bfloat16)), lat_idx)
    cos_fwd, sin_fwd, inverse = (jnp.asarray(t.astype(jnp.bfloat16)) for t in fourier_tables(all_cols))
    l_max = pick(lmax, section_idx)
    m_max = pick(mmax, section_idx)
    keep = (
        (jnp.arange(n_degrees, dtype=jnp.int32) < l_max)[:, None] & (m_global < m_max)[None, :]
    ).astype(jnp.float32)[:, :, None]

    def run_block(tokens, tick):
        block_idx = pick(plan[tick], section_idx)
        cut = pick(cutoff, tick - section_idx + n_section - 1)
        gains = pick(norm_gains[0], block_idx)
        filt = pick(filters[0], block_idx)
        weight_in = pick(w_in[0], block_idx)
        weight_out = pick(w_out[0], block_idx)
        onehot = (jnp.arange(cutoff_table.shape[0], dtype=jnp.int32) == cut).astype(jnp.float32)
        embed = jnp.dot(onehot, cutoff_table, precision=highest)
        base = tokens.astype(jnp.float32) + embed
        normed = layer_norm(base, gains[0]).astype(jnp.bfloat16)
        by_lon = lax.all_to_all(normed, "lon", split_axis=2, concat_axis=1, tiled=True)
        wide = by_lon
        real_part = jnp.einsum("jkc,km->jmc", wide, cos_fwd, preferred_element_type=jnp.float32)
        imag_part = jnp.einsum("jkc,km->jmc", wide, sin_fwd, preferred_element_type=jnp.float32)
        spectrum = jnp.stack([real_part, imag_part], 1).astype(jnp.bfloat16)
        by_mode = lax.all_to_all(spectrum, "lat", split_axis=2, concat_axis=0, tiled=True)
        coeff = jnp.einsum(
            "lmj,jrmc->rlmc", weighted, by_mode, preferred_element_type=jnp.float32
        )
        filt_re = filt[0][:, None, :]
        filt_im = filt[1][:, None, :]
        out_re = keep * (coeff[0] * filt_re - coeff[1] * filt_im)
        out_im = keep * (coeff[0] * filt_im + coeff[1] * filt_re)
        synthesis = jnp.einsum(
            "lmj,rlmc->jrmc", plain, jnp.stack([out_re, out_im], 0).astype(jnp.bfloat16), preferred_element_type=jnp.float32
        ).astype(jnp.bfloat16)
        by_row = lax.all_to_all(synthesis, "lat", split_axis=0, concat_axis=2, tiled=True)
        spectral = jnp.einsum(
            "jrmc,rmk->jkc", by_row, inverse, preferred_element_type=jnp.float32
        ).astype(jnp.bfloat16)
        spectral = lax.all_to_all(spectral, "lon", split_axis=1, concat_axis=2, tiled=True)
        mixed = base + spectral.astype(jnp.float32)
        normed_two = layer_norm(mixed, gains[1]).astype(jnp.bfloat16)
        flat = normed_two.reshape(n_rows * n_cols, width)
        before_act = jnp.dot(
            flat,
            lax.all_gather(weight_in, "lat", axis=0, tiled=True),
            preferred_element_type=jnp.float32,
        )
        hidden = jax.nn.gelu(before_act).astype(jnp.bfloat16)
        projected = lax.dot_general(
            hidden,
            lax.all_gather(weight_out, "lat", axis=0, tiled=True),
            (((1,), (1,)), ((), ())),
            preferred_element_type=jnp.float32,
        )
        result = mixed + projected.reshape(mixed.shape)
        return result.astype(jnp.bfloat16)

    first_out = run_block(state[0], 0)
    handed = passed_along(first_out, "section", 1)
    entering = jnp.where(section_idx == 0, fresh, handed)
    second_out = run_block(entering, 1)
    return (first_out[None], second_out[None])


def solution(mesh):
    return jax.shard_map(
        local,
        mesh=mesh,
        in_specs=(
            P("section", "lat", "lon", None),
            P("lat", "lon", None),
            P(),
            P(),
            P(),
            P(),
            P(),
            P("section", None, None, None),
            P("section", None, None, None, "lon"),
            P("section", None, "lat", None),
            P("section", None, "lat", None),
        ),
        out_specs=(P("section", "lat", "lon", None), P("section", "lat", "lon", None)),
        check_vma=False,
    )
```

```python
import functools
import math

import jax
import jax.numpy as jnp
import numpy as np
from jax import lax
from jax.experimental import pallas as pl
from jax.experimental.pallas import tpu as pltpu
from jax.sharding import PartitionSpec as P

MM = 96
MESH = pl.DeviceIdType.MESH
BF16 = jnp.bfloat16
F32 = jnp.float32
VMEM = 60 * 1024 * 1024
LON_PAD = 96
MODE_PAD = 16
GROUPS = ((0, 4), (4, 3))


def passed_along(value, axis, steps):
    count = lax.axis_size(axis)
    leading, last = (max(0, -steps), min(count, count - steps))
    return lax.ppermute(value, axis, [(source, source + steps) for source in range(leading, last)])


def legendre_table(n_orders, n_rows, n_degrees):
    theta = math.pi * (np.arange(n_rows) + 0.5) / n_rows
    cosine, sine = np.cos(theta), np.sin(theta)
    table = np.zeros((n_degrees, n_orders, n_rows))
    for m in range(n_orders):
        log_start = (
            0.5 * math.log((2.0 * m + 1.0) / (4.0 * math.pi))
            + math.lgamma(m + 0.5) - math.lgamma(0.5) - math.lgamma(m + 1.0)
        )
        table[m, m] = np.exp(log_start + m * np.log(sine))
        for l in range(m + 1, n_degrees):
            coef_a = math.sqrt((4.0 * l * l - 1.0) / (l * l - m * m))
            coef_b = math.sqrt(max((l - 1.0) ** 2 - m * m, 0.0) / max(4.0 * (l - 1.0) ** 2 - 1.0, 1.0))
            before = table[l - 2, m] if l - 2 >= m else 0.0
            table[l, m] = coef_a * (cosine * table[l - 1, m] - coef_b * before)
    quad = 2.0 * math.pi * (math.pi / n_rows) * sine
    return table, table * quad


def spectral_tables(n_lat, n_lon, n_rows, n_cols, n_degrees):
    m_local = MM // n_lat
    all_cols = n_cols * n_lon
    phase = 2.0 * math.pi * ((np.arange(all_cols)[:, None] * np.arange(MM)[None, :]) % all_cols) / all_cols
    weight = np.where(np.arange(MM) == 0, 1.0, 2.0)
    forward = np.zeros((n_lat, MODE_PAD, n_lon, LON_PAD))
    inverse = np.zeros((n_lon, LON_PAD, n_lat, MODE_PAD))
    parts = ((np.cos(phase) / all_cols, weight * np.cos(phase)), (-np.sin(phase) / all_cols, -weight * np.sin(phase)))
    for r, (fwd, inv) in enumerate(parts):
        fwd = fwd.reshape(n_lon, n_cols, n_lat, m_local)
        inv = inv.reshape(n_lon, n_cols, n_lat, m_local)
        forward[:, r * m_local : (r + 1) * m_local, :, :n_cols] = fwd.transpose(2, 3, 0, 1)
        inverse[:, :n_cols, :, r * m_local : (r + 1) * m_local] = inv
    forward = forward.reshape(n_lat * MODE_PAD, n_lon * LON_PAD)
    inverse = inverse.reshape(n_lon * LON_PAD, n_lat * MODE_PAD)
    plain, weighted = legendre_table(MM, n_rows * n_lat, n_degrees)
    split = (n_degrees, n_lat, m_local, n_lat, n_rows)
    weighted = weighted.reshape(split).transpose(1, 2, 0, 3, 4).reshape(n_lat, m_local, n_degrees, n_lat * n_rows)
    padded = np.zeros((n_lat, m_local, n_lat, 8, n_degrees))
    padded[:, :, :, :n_rows] = plain.reshape(split).transpose(1, 2, 3, 4, 0)
    padded = padded.reshape(n_lat, m_local, n_lat * 8, n_degrees)
    return tuple(t.astype(BF16) for t in (forward, inverse, weighted, padded))


def layer_norm(values, gain):
    scale = 1.0 / values.shape[-1]
    center = values - jnp.sum(values, axis=-1, keepdims=True) * scale
    spread = jnp.sum(center * center, axis=-1, keepdims=True) * scale
    return center * lax.rsqrt(spread + 1e-05) * gain


def lon_peer(me, d):
    return lax.rem(me // 2 + d // 2, 2) * 2 + lax.rem(lax.rem(me, 2) + d % 2, 2)


def spec_kernel(
    tick, n_section, plan, cutoff, lmax, mmax, tok, cut_table, gains, filters, fwd, inv, leg_hbm, legt_hbm,
    v_out, own_out, sib_out,
    norm, x_all, spec, y_all, y_f32, f_f32, back, z_all, o_all, r_all, vbuf, nbuf, leg, legt,
    a_send, a_recv, b_send, b_recv, c_send, c_recv, d_send, d_recv, n_send, n_recv, loc,
):
    section, lat, lon = (lax.axis_index(a) for a in ("section", "lat", "lon"))
    n_lat = spec.shape[0]
    n_rows, n_cols, width = tok.shape
    n_degrees, part = filters.shape[3], filters.shape[4]
    m_local = leg.shape[0]
    half = part // 2
    sibling = lon_peer(lon, 1)

    barrier = pltpu.get_barrier_semaphore()
    for d in (1, 2, 3):
        pl.semaphore_signal(barrier, inc=1, device_id={"lon": lon_peer(lon, d)}, device_id_type=MESH)

    def greet(d, carry):
        pl.semaphore_signal(barrier, inc=1, device_id={"lat": lax.rem(lat + d, n_lat)}, device_id_type=MESH)
        return carry

    lax.fori_loop(1, n_lat, greet, 0)
    get_leg = pltpu.make_async_copy(leg_hbm.at[lat], leg, loc.at[0])
    get_legt = pltpu.make_async_copy(legt_hbm.at[lat], legt, loc.at[1])
    get_leg.start()
    get_legt.start()

    block = plan[tick, section]
    cut = cutoff[tick - section + n_section - 1]
    l_max, m_max = lmax[section], mmax[section]
    embed = cut_table[pl.ds(cut, 1), :]
    gain_one = gains[0, block, 0:1, :]
    gain_two = gains[0, block, 1:2, :]
    norm[:, :, LON_PAD - 16 :, :] = jnp.zeros((4, n_rows, 16, part), BF16)
    f_f32[...] = jnp.zeros_like(f_f32)
    pl.semaphore_wait(barrier, 3 + n_lat - 1)

    def send_a(j, d):
        peer = lon_peer(lon, d)
        return pltpu.make_async_remote_copy(
            src_ref=norm.at[peer, j], dst_ref=x_all.at[lon, j], send_sem=a_send.at[d, j],
            recv_sem=a_recv.at[d, j], device_id={"lon": peer}, device_id_type=MESH)

    def take_a(j, d):
        peer = lon_peer(lon, d)
        return pltpu.make_async_remote_copy(
            src_ref=norm.at[peer, j], dst_ref=x_all.at[peer, j], send_sem=a_send.at[d, j],
            recv_sem=a_recv.at[d, j], device_id={"lon": peer}, device_id_type=MESH)

    def first_norm(j, carry):
        base = tok[j].astype(F32) + embed
        out = layer_norm(base, gain_one).astype(BF16)
        for q in range(4):
            norm[q, j, 0:n_cols, :] = out[:, q * part : (q + 1) * part]
        for d in (2, 3, 1):
            send_a(j, d).start()
        x_all[lon, j] = norm[lon, j]
        return carry

    lax.fori_loop(0, n_rows, first_norm, 0)

    def moved(src, dst, send, recv, mine, slot, g, d):
        first, count = GROUPS[g]
        peer = lax.rem(lat + d, n_lat)
        origin = lax.rem(lat - d + n_lat, n_lat)
        where = lat if mine else origin
        return pltpu.make_async_remote_copy(
            src_ref=src.at[peer, pl.ds(first, count)], dst_ref=dst.at[where, pl.ds(first, count)],
            send_sem=send.at[g, d], recv_sem=recv.at[g, d], device_id={"lat": peer}, device_id_type=MESH)

    def zonal(j, carry):
        for d in (1, 2, 3):
            take_a(j, d).wait_recv()
        wide = x_all[:, j].reshape(4 * LON_PAD, part)
        out = jnp.dot(fwd[...], wide, preferred_element_type=F32)
        spec[:, j] = out.astype(BF16).reshape(n_lat, MODE_PAD, part)
        return carry

    for g, (first, count) in enumerate(GROUPS):
        lax.fori_loop(first, first + count, zonal, 0)

        def send_b(d, carry, g=g):
            moved(spec, y_all, b_send, b_recv, True, 0, g, d).start()
            return carry

        lax.fori_loop(1, n_lat, send_b, 0)

    rows = n_rows * MODE_PAD

    def widen(src, value):
        at = pl.multiple_of(src * rows, 16)
        value = value.reshape(rows, part).astype(F32)
        y_f32[0, pl.ds(at, rows), :] = value[:, :half]
        y_f32[1, pl.ds(at, rows), :] = value[:, half:]

    widen(lat, spec[lat])

    def take_b(d, carry):
        for g in range(len(GROUPS)):
            moved(spec, y_all, b_send, b_recv, False, 0, g, d).wait_recv()
        origin = lax.rem(lat - d + n_lat, n_lat)
        widen(origin, y_all[origin])
        return carry

    get_leg.wait()
    get_legt.wait()
    lax.fori_loop(1, n_lat, take_b, 0)

    fil_re = filters[0, block, 0]
    fil_im = filters[0, block, 1]
    degree = lax.broadcasted_iota(jnp.int32, (n_degrees, part), 0)
    n_lines = n_lat * n_rows
    for m in range(m_local):
        pieces = [y_f32[h, pl.ds(r * m_local + m, n_lines, stride=MODE_PAD), :] for r in (0, 1) for h in (0, 1)]
        column = jnp.concatenate(pieces, axis=1).astype(BF16)
        coeff = jnp.dot(leg[m], column, preferred_element_type=F32)
        co_re, co_im = coeff[:, :part], coeff[:, part:]
        order = lat * m_local + m
        keep = (degree < l_max) & (jnp.full((n_degrees, part), order, jnp.int32) < m_max)
        out_re = jnp.where(keep, co_re * fil_re - co_im * fil_im, 0.0)
        out_im = jnp.where(keep, co_re * fil_im + co_im * fil_re, 0.0)
        out = jnp.concatenate([out_re, out_im], axis=1).astype(BF16)
        lines = jnp.dot(legt[m], out, preferred_element_type=F32)
        for r in (0, 1):
            for h in (0, 1):
                at = (2 * r + h) * half
                f_f32[h, pl.ds(r * m_local + m, n_lat * 8, stride=MODE_PAD), :] = lines[:, at : at + half]

    def narrow(peer):
        at = pl.multiple_of(peer * (8 * MODE_PAD), 16)
        value = jnp.concatenate([f_f32[h, pl.ds(at, rows), :] for h in (0, 1)], axis=1)
        return value.astype(BF16).reshape(n_rows, MODE_PAD, part)

    def send_c(d, carry):
        peer = lax.rem(lat + d, n_lat)
        back[peer] = narrow(peer)
        for g in range(len(GROUPS)):
            moved(back, z_all, c_send, c_recv, True, 0, g, d).start()
        return carry

    lax.fori_loop(1, n_lat, send_c, 0)
    z_all[lat] = narrow(lat)

    def send_d(j, d):
        peer = lon_peer(lon, d)
        return pltpu.make_async_remote_copy(
            src_ref=o_all.at[peer, j], dst_ref=r_all.at[lon, j], send_sem=d_send.at[d, j],
            recv_sem=d_recv.at[d, j], device_id={"lon": peer}, device_id_type=MESH)

    def take_d(j, d):
        peer = lon_peer(lon, d)
        return pltpu.make_async_remote_copy(
            src_ref=o_all.at[peer, j], dst_ref=r_all.at[peer, j], send_sem=d_send.at[d, j],
            recv_sem=d_recv.at[d, j], device_id={"lon": peer}, device_id_type=MESH)

    def unzonal(j, carry):
        modes = z_all[:, j].reshape(n_lat * MODE_PAD, part)
        out = jnp.dot(inv[...], modes, preferred_element_type=F32)
        o_all[:, j] = out.astype(BF16).reshape(4, LON_PAD, part)
        for d in (2, 3, 1):
            send_d(j, d).start()
        r_all[lon, j] = o_all[lon, j]
        return carry

    for g, (first, count) in enumerate(GROUPS):

        def take_c(d, carry, g=g):
            moved(back, z_all, c_send, c_recv, False, 0, g, d).wait_recv()
            return carry

        lax.fori_loop(1, n_lat, take_c, 0)
        lax.fori_loop(first, first + count, unzonal, 0)

    def put_v(j):
        return pltpu.make_async_copy(vbuf.at[j], v_out.at[j], loc.at[2 + j])

    def put_own(j):
        return pltpu.make_async_copy(nbuf.at[j], own_out.at[j], loc.at[2 + n_rows + j])

    def put_sib(j):
        return pltpu.make_async_remote_copy(
            src_ref=nbuf.at[j], dst_ref=sib_out.at[j], send_sem=n_send.at[j], recv_sem=n_recv.at[j],
            device_id={"lon": sibling}, device_id_type=MESH)

    def second_norm(j, carry):
        for d in (1, 2, 3):
            take_d(j, d).wait_recv()
        spectral = jnp.concatenate([r_all[q, j, 0:n_cols, :] for q in range(4)], axis=1).astype(F32)
        mixed = tok[j].astype(F32) + embed + spectral
        vbuf[j] = mixed
        nbuf[j, 0:n_cols, :] = layer_norm(mixed, gain_two).astype(BF16)
        put_sib(j).start()
        put_v(j).start()
        put_own(j).start()
        return carry

    nbuf[:, LON_PAD - 16 :, :] = jnp.zeros((n_rows, 16, width), BF16)
    lax.fori_loop(0, n_rows, second_norm, 0)

    def finish_rows(j, carry):
        for d in (1, 2, 3):
            send_a(j, d).wait_send()
            send_d(j, d).wait_send()
        put_v(j).wait()
        put_own(j).wait()
        put_sib(j).wait()
        return carry

    def finish_lat(d, carry):
        for g in range(len(GROUPS)):
            moved(spec, y_all, b_send, b_recv, True, 0, g, d).wait_send()
            moved(back, z_all, c_send, c_recv, True, 0, g, d).wait_send()
        return carry

    lax.fori_loop(1, n_lat, finish_lat, 0)
    lax.fori_loop(0, n_rows, finish_rows, 0)


def spectral_part(tick, n_section, plan, cutoff, lmax, mmax, tokens, cut_table, gains, filters, tables):
    n_rows, n_cols, width = tokens.shape
    fwd, inv, leg, legt = tables
    n_lat, m_local, n_degrees, n_lines = leg.shape
    part = filters.shape[4]
    smem = pl.BlockSpec(memory_space=pltpu.SMEM)
    vmem = pl.BlockSpec(memory_space=pltpu.VMEM)
    anys = pl.BlockSpec(memory_space=pltpu.HBM)
    dma = pltpu.SemaphoreType.DMA
    lonwise = pltpu.VMEM((4, n_rows, LON_PAD, part), BF16)
    latwise = pltpu.VMEM((n_lat, n_rows, MODE_PAD, part), BF16)
    n_groups = len(GROUPS)
    return pl.pallas_call(
        functools.partial(spec_kernel, tick, n_section),
        out_shape=(
            jax.ShapeDtypeStruct((n_rows, n_cols, width), F32),
            jax.ShapeDtypeStruct((n_rows, LON_PAD, width), BF16),
            jax.ShapeDtypeStruct((n_rows, LON_PAD, width), BF16),
        ),
        in_specs=[smem] * 4 + [vmem] * 6 + [anys] * 2,
        out_specs=(anys, anys, anys),
        scratch_shapes=[
            lonwise, lonwise, latwise, latwise,
            pltpu.VMEM((2, n_lines * MODE_PAD, part // 2), F32),
            pltpu.VMEM((2, n_lat * 8 * MODE_PAD, part // 2), F32),
            latwise, latwise, lonwise, lonwise,
            pltpu.VMEM((n_rows, n_cols, width), F32),
            pltpu.VMEM((n_rows, LON_PAD, width), BF16),
            pltpu.VMEM(leg.shape[1:], BF16),
            pltpu.VMEM(legt.shape[1:], BF16),
            dma((4, n_rows)), dma((4, n_rows)),
            dma((n_groups, n_lat)), dma((n_groups, n_lat)),
            dma((n_groups, n_lat)), dma((n_groups, n_lat)),
            dma((4, n_rows)), dma((4, n_rows)),
            dma((n_rows,)), dma((n_rows,)),
            dma((2 + 2 * n_rows,)),
        ],
        compiler_params=pltpu.CompilerParams(
            collective_id=2 * tick, has_side_effects=True, vmem_limit_bytes=VMEM),
        cost_estimate=pl.CostEstimate(flops=5 * 10**10, bytes_accessed=10**7, transcendentals=0),
    )(plan, cutoff, lmax, mmax, tokens, cut_table, gains, filters, fwd, inv, leg, legt)


CHUNKS = 4


def mlp_kernel(
    v_hbm, own_hbm, sib_hbm, w_hbm, out_hbm,
    x_all, wi, wo, acc, given, taken, vbuf, obuf, x_sem, w_sem, v_sem, o_sem, p_send, p_recv,
):
    lon = lax.axis_index("lon")
    sibling = lon_peer(lon, 1)
    n_rows, n_cols, width = v_hbm.shape
    ff = wi.shape[3]
    shard = w_hbm.shape[1] // 2

    barrier = pltpu.get_barrier_semaphore()
    pl.semaphore_signal(barrier, inc=1, device_id={"lon": sibling}, device_id_type=MESH)

    get_x = [
        pltpu.make_async_copy(ref.at[pl.ds(first, count)], x_all.at[pl.ds(n_rows * k + first, count)], x_sem.at[2 * k + g])
        for k, ref in enumerate((sib_hbm, own_hbm))
        for g, (first, count) in enumerate(GROUPS)
    ]

    def get_wi(c):
        return pltpu.make_async_copy(w_hbm.at[:, pl.ds(0, shard), pl.ds(c * ff, ff)], wi.at[c], w_sem.at[0, c])

    def get_wo(c):
        return pltpu.make_async_copy(w_hbm.at[:, pl.ds(shard, shard), pl.ds(c * ff, ff)], wo.at[c], w_sem.at[1, c])

    get_v = pltpu.make_async_copy(v_hbm, vbuf, v_sem)
    get_x[0].start()
    for c in range(CHUNKS):
        get_wi(c).start()
        get_wo(c).start()
        if c == 0:
            get_x[1].start()
    get_x[2].start()
    get_x[3].start()
    get_v.start()
    pl.semaphore_wait(barrier, 1)

    def send(g):
        first, count = GROUPS[g]
        return pltpu.make_async_remote_copy(
            src_ref=given.at[pl.ds(first, count)], dst_ref=taken.at[pl.ds(first, count)],
            send_sem=p_send.at[g], recv_sem=p_recv.at[g], device_id={"lon": sibling}, device_id_type=MESH)

    def put(j):
        return pltpu.make_async_copy(obuf.at[j], out_hbm.at[j], o_sem.at[j])

    for tile in range(4):
        k, g = tile // 2, tile % 2
        first, count = GROUPS[g]
        size = count * LON_PAD
        get_x[tile].wait()

        def body(c, carry, tile=tile, at=n_rows * k + first, count=count, size=size):
            if tile == 0:
                get_wi(c).wait()
                get_wo(c).wait()
            x = x_all[pl.ds(at, count)].reshape(size, width)
            h = jax.nn.gelu(jnp.dot(x, wi[c].reshape(width, ff), preferred_element_type=F32)).astype(BF16)
            out = lax.dot_general(h, wo[c].reshape(width, ff), (((1,), (1,)), ((), ())), preferred_element_type=F32)
            old = jnp.where(c == 0, 0.0, acc[0:size, :])
            acc[0:size, :] = old + out
            return carry

        lax.fori_loop(0, CHUNKS, body, 0)
        total = acc[0:size, :].reshape(count, LON_PAD, width)
        if k == 0:
            given[pl.ds(first, count)] = total.astype(BF16)
            send(g).start()
        else:
            if g == 0:
                get_v.wait()
            send(g).wait_recv()
            for i in range(count):
                j = first + i
                other = taken[j, 0:n_cols, :].astype(F32)
                obuf[j] = (vbuf[j] + (total[i, 0:n_cols, :] + other)).astype(BF16)
                put(j).start()
    for j in range(n_rows):
        put(j).wait()
    for g in range(2):
        send(g).wait_send()


def mlp_part(tick, v, own, sib, weights):
    n_rows, n_cols, width = v.shape
    n_lat, shard, ff = weights.shape
    shard, ff = shard // 2, ff // CHUNKS
    anys = pl.BlockSpec(memory_space=pltpu.HBM)
    dma = pltpu.SemaphoreType.DMA
    most = max(count for _, count in GROUPS)
    return pl.pallas_call(
        mlp_kernel,
        out_shape=jax.ShapeDtypeStruct((n_rows, n_cols, width), BF16),
        in_specs=[anys] * 4,
        out_specs=anys,
        scratch_shapes=[
            pltpu.VMEM((2 * n_rows, LON_PAD, width), BF16),
            pltpu.VMEM((CHUNKS, n_lat, shard, ff), BF16),
            pltpu.VMEM((CHUNKS, n_lat, shard, ff), BF16),
            pltpu.VMEM((most * LON_PAD, width), F32),
            pltpu.VMEM((n_rows, LON_PAD, width), BF16),
            pltpu.VMEM((n_rows, LON_PAD, width), BF16),
            pltpu.VMEM((n_rows, n_cols, width), F32),
            pltpu.VMEM((n_rows, n_cols, width), BF16),
            dma((4,)), dma((2, CHUNKS)), dma(()), dma((n_rows,)), dma((2,)), dma((2,)),
        ],
        compiler_params=pltpu.CompilerParams(
            collective_id=2 * tick + 1, has_side_effects=True, vmem_limit_bytes=VMEM),
        cost_estimate=pl.CostEstimate(flops=10**10, bytes_accessed=10**7, transcendentals=0),
    )(v, own, sib, weights)


def local(state, fresh, cutoff, plan, lmax, mmax, cutoff_table, norm_gains, filters, w_in, w_out):
    section_idx = lax.axis_index("section")
    n_section = lax.axis_size("section")
    n_lat = lax.axis_size("lat")
    n_lon = lax.axis_size("lon")
    n_rows, n_cols, width = fresh.shape
    n_degrees = filters.shape[3]
    tables = [jnp.asarray(t) for t in spectral_tables(n_lat, n_lon, n_rows, n_cols, n_degrees)]
    core = lax.rem(lax.axis_index("lon"), 2)
    ff_half = w_in.shape[3] // 2

    def gathered(tick):
        block = lax.dynamic_index_in_dim(plan[tick], section_idx, 0, keepdims=False)
        zero = jnp.int32(0)
        mine = [
            lax.dynamic_slice(weight, (zero, block, zero, core * ff_half), (1, 1, weight.shape[2], ff_half))[0, 0]
            for weight in (w_in, w_out)
        ]
        return lax.all_gather(jnp.concatenate(mine, 0), "lat", axis=0)

    weights = [gathered(tick) for tick in (0, 1)]

    def run_block(tokens, tick):
        v, own, sib = spectral_part(
            tick, n_section, plan, cutoff, lmax, mmax, tokens, cutoff_table, norm_gains, filters, tables)
        return mlp_part(tick, v, own, sib, weights[tick])

    first_out = run_block(state[0], 0)
    handed = passed_along(first_out, "section", 1)
    entering = jnp.where(section_idx == 0, fresh, handed)
    second_out = run_block(entering, 1)
    return (first_out[None], second_out[None])


def solution(mesh):
    return jax.shard_map(
        local,
        mesh=mesh,
        in_specs=(
            P("section", "lat", "lon", None),
            P("lat", "lon", None),
            P(),
            P(),
            P(),
            P(),
            P(),
            P("section", None, None, None),
            P("section", None, None, None, "lon"),
            P("section", None, "lat", None),
            P("section", None, "lat", None),
        ),
        out_specs=(P("section", "lat", "lon", None), P("section", "lat", "lon", None)),
        check_vma=False,
    )
```

```python
import functools
import math

import jax
import jax.numpy as jnp
import numpy as np
from jax import lax
from jax.experimental import pallas as pl
from jax.experimental.pallas import tpu as pltpu
from jax.sharding import PartitionSpec as P

MM = 96
MESH = pl.DeviceIdType.MESH
BF16 = jnp.bfloat16
F32 = jnp.float32
VMEM = 60 * 1024 * 1024
LON_PAD = 96
MODE_PAD = 16
GROUPS = ((0, 4), (4, 3))
ROWS = ((0, 2), (2, 2), (4, 3))


def passed_along(value, axis, steps):
    count = lax.axis_size(axis)
    leading, last = (max(0, -steps), min(count, count - steps))
    return lax.ppermute(value, axis, [(source, source + steps) for source in range(leading, last)])


def legendre_table(n_orders, n_rows, n_degrees):
    theta = math.pi * (np.arange(n_rows) + 0.5) / n_rows
    cosine, sine = np.cos(theta), np.sin(theta)
    table = np.zeros((n_degrees, n_orders, n_rows))
    for m in range(n_orders):
        log_start = (
            0.5 * math.log((2.0 * m + 1.0) / (4.0 * math.pi))
            + math.lgamma(m + 0.5) - math.lgamma(0.5) - math.lgamma(m + 1.0)
        )
        table[m, m] = np.exp(log_start + m * np.log(sine))
        for l in range(m + 1, n_degrees):
            coef_a = math.sqrt((4.0 * l * l - 1.0) / (l * l - m * m))
            coef_b = math.sqrt(max((l - 1.0) ** 2 - m * m, 0.0) / max(4.0 * (l - 1.0) ** 2 - 1.0, 1.0))
            before = table[l - 2, m] if l - 2 >= m else 0.0
            table[l, m] = coef_a * (cosine * table[l - 1, m] - coef_b * before)
    quad = 2.0 * math.pi * (math.pi / n_rows) * sine
    return table, table * quad


def spectral_tables(n_lat, n_lon, n_rows, n_cols, n_degrees):
    m_local = MM // n_lat
    all_cols = n_cols * n_lon
    phase = 2.0 * math.pi * ((np.arange(all_cols)[:, None] * np.arange(MM)[None, :]) % all_cols) / all_cols
    weight = np.where(np.arange(MM) == 0, 1.0, 2.0)
    forward = np.zeros((n_lat, MODE_PAD, n_lon, LON_PAD))
    inverse = np.zeros((n_lon, LON_PAD, n_lat, MODE_PAD))
    parts = ((np.cos(phase) / all_cols, weight * np.cos(phase)), (-np.sin(phase) / all_cols, -weight * np.sin(phase)))
    for r, (fwd, inv) in enumerate(parts):
        fwd = fwd.reshape(n_lon, n_cols, n_lat, m_local)
        inv = inv.reshape(n_lon, n_cols, n_lat, m_local)
        forward[:, r * m_local : (r + 1) * m_local, :, :n_cols] = fwd.transpose(2, 3, 0, 1)
        inverse[:, :n_cols, :, r * m_local : (r + 1) * m_local] = inv
    forward = forward.reshape(n_lat * MODE_PAD, n_lon * LON_PAD)
    inverse = inverse.reshape(n_lon * LON_PAD, n_lat * MODE_PAD)
    plain, weighted = legendre_table(MM, n_rows * n_lat, n_degrees)
    split = (n_degrees, n_lat, m_local, n_lat, n_rows)
    weighted = weighted.reshape(split).transpose(1, 2, 0, 3, 4).reshape(n_lat, m_local, n_degrees, n_lat * n_rows)
    padded = np.zeros((n_lat, m_local, n_lat, 8, n_degrees))
    padded[:, :, :, :n_rows] = plain.reshape(split).transpose(1, 2, 3, 4, 0)
    padded = padded.reshape(n_lat, m_local, n_lat * 8, n_degrees)
    return tuple(t.astype(BF16) for t in (forward, inverse, weighted, padded))


def layer_norm(values, gain):
    scale = 1.0 / values.shape[-1]
    center = values - jnp.sum(values, axis=-1, keepdims=True) * scale
    spread = jnp.sum(center * center, axis=-1, keepdims=True) * scale
    return center * lax.rsqrt(spread + 1e-05) * gain


def lon_peer(me, d):
    return lax.rem(me // 2 + d // 2, 2) * 2 + lax.rem(lax.rem(me, 2) + d % 2, 2)


def spec_kernel(
    tick, n_section, plan, cutoff, lmax, mmax, *refs,
):
    if tick == 0:
        tok_hbm, prior_hbm, *refs = refs
    else:
        tok_hbm, prior_hbm, other_gains, x_next, *refs = refs
    cut_table, gains, filters, fwd, inv, leg_hbm, legt_hbm, v_out, own_out, sib_out, *refs = refs
    if tick == 0:
        x_next, *refs = refs
    (
        tok, prior, norm, ahead, x_all, spec, y_all, y_f32, f_f32, back, z_all, o_all, r_all, vbuf, nbuf, leg, legt,
        a_send, a_recv, e_send, f_recv, t_send, t_recv, b_send, b_recv, c_send, c_recv, d_send, d_recv, n_send, n_recv, loc, row_in, next_sem,
    ) = refs
    section, lat, lon = (lax.axis_index(a) for a in ("section", "lat", "lon"))
    n_lat = spec.shape[1]
    n_rows, n_cols, width = tok.shape
    n_degrees, part = filters.shape[3], filters.shape[4]
    m_local = leg.shape[0]
    half = part // 2
    sibling = lon_peer(lon, 1)
    handing = tick > 0
    first_section = section == 0

    barrier = pltpu.get_barrier_semaphore()
    greeted = 3 + n_lat - 1
    for d in (1, 2, 3):
        pl.semaphore_signal(barrier, inc=1, device_id={"lon": lon_peer(lon, d)}, device_id_type=MESH)
    if handing:
        greeted += 4
        for q in range(4):
            pl.semaphore_signal(barrier, inc=1, device_id={"section": 1 - section, "lon": q}, device_id_type=MESH)

    def greet(d, carry):
        pl.semaphore_signal(barrier, inc=1, device_id={"lat": lax.rem(lat + d, n_lat)}, device_id_type=MESH)
        return carry

    lax.fori_loop(1, n_lat, greet, 0)

    def get_tok(j):
        return pltpu.make_async_copy(tok_hbm.at[j], tok.at[j], row_in.at[0, j])

    def get_prior(j):
        return pltpu.make_async_copy(prior_hbm.at[j], prior.at[j], row_in.at[1, j])

    def get_next(h):
        return pltpu.make_async_copy(x_next.at[h], x_all.at[h], next_sem.at[h])

    def put_next(h):
        return pltpu.make_async_copy(ahead.at[h, lon], x_next.at[h, lon], next_sem.at[h])

    def over_rows(step):
        def body(j, carry):
            step(j)
            return carry

        lax.fori_loop(0, n_rows, body, 0)

    if handing:

        @pl.when(first_section)
        def _():
            over_rows(lambda j: get_prior(j).start())
            for h in (0, 1):
                get_next(h).start()
            over_rows(lambda j: get_tok(j).start())
    else:
        over_rows(lambda j: get_tok(j).start())

        @pl.when(first_section)
        def _():
            over_rows(lambda j: get_prior(j).start())
    get_leg = pltpu.make_async_copy(leg_hbm.at[lat], leg, loc.at[0])
    get_legt = pltpu.make_async_copy(legt_hbm.at[lat], legt, loc.at[1])
    get_leg.start()
    get_legt.start()

    block = plan[tick, section]
    cut = cutoff[tick - section + n_section - 1]
    l_max, m_max = lmax[section], mmax[section]
    embed = cut_table[pl.ds(cut, 1), :]
    gain_one = gains[0, block, 0:1, :]
    gain_two = gains[0, block, 1:2, :]
    pad = jnp.zeros((2, 4, n_rows, 16, half), BF16)
    ahead[:, :, :, LON_PAD - 16 :, :] = pad
    if not handing:
        norm[:, :, :, LON_PAD - 16 :, :] = pad
    f_f32[...] = jnp.zeros_like(f_f32)
    nbuf[:, LON_PAD - 16 :, :] = jnp.zeros((n_rows, 16, width), BF16)
    pl.semaphore_wait(barrier, greeted)

    def copy_a(h, j, d, sending):
        peer = lon_peer(lon, d)
        slot = lon if sending else peer
        return pltpu.make_async_remote_copy(
            src_ref=norm.at[h, peer, j] if sending else x_all.at[h, slot, j], dst_ref=x_all.at[h, slot, j], send_sem=a_send.at[h, d, j],
            recv_sem=a_recv.at[h, d, j], device_id={"lon": peer}, device_id_type=MESH)

    def copy_e(h, j, d):
        peer = lon_peer(lon, d)
        return pltpu.make_async_remote_copy(
            src_ref=ahead.at[h, peer, j], dst_ref=x_all.at[h, lon, j], send_sem=e_send.at[h, d, j],
            recv_sem=a_recv.at[h, d, j], device_id={"section": 1 - section, "lon": peer}, device_id_type=MESH)

    def copy_f(h, j, d, sending):
        peer = lon_peer(lon, d)
        slot = lon if sending else peer
        return pltpu.make_async_remote_copy(
            src_ref=ahead.at[h, peer, j], dst_ref=x_next.at[h, slot, j], send_sem=e_send.at[h, d, j],
            recv_sem=f_recv.at[h, d, j], device_id={"lon": peer}, device_id_type=MESH)

    def copy_t(j):
        return pltpu.make_async_remote_copy(
            src_ref=prior.at[j], dst_ref=tok.at[j], send_sem=t_send.at[j], recv_sem=t_recv.at[j],
            device_id={"section": 1 - section}, device_id_type=MESH)

    def split_into(dst, j, out):
        for q in range(4):
            for h in (0, 1):
                at = q * part + h * half
                dst[h, q, j, 0:n_cols, :] = out[:, at : at + half]

    def first_norm(j):
        get_tok(j).wait()
        split_into(norm, j, layer_norm(tok[j].astype(F32) + embed, gain_one).astype(BF16))
        for d in (2, 3, 1):
            copy_a(0, j, d, True).start()
        for h in (0, 1):
            x_all[h, lon, j] = norm[h, lon, j]

    def first_norm_rest(j):
        for d in (2, 3, 1):
            copy_a(1, j, d, True).start()

    if handing:

        @pl.when(first_section)
        def _():
            next_block = plan[tick, 1]
            next_embed = cut_table[pl.ds(cutoff[tick - 1 + n_section - 1], 1), :]
            next_gain = other_gains[0, next_block, 0:1, :]

            def norm_ahead(j):
                get_prior(j).wait()
                split_into(ahead, j, layer_norm(prior[j].astype(F32) + next_embed, next_gain).astype(BF16))
                for d in range(4):
                    copy_e(0, j, d).start()

            def norm_ahead_rest(j):
                for d in range(4):
                    copy_e(1, j, d).start()

            over_rows(norm_ahead)
            over_rows(norm_ahead_rest)
            over_rows(lambda j: copy_t(j).start())
    else:
        over_rows(first_norm)
        over_rows(first_norm_rest)

        @pl.when(first_section)
        def _():
            next_block = plan[tick + 1, 0]
            next_embed = cut_table[pl.ds(cutoff[tick + 1 + n_section - 1], 1), :]
            next_gain = gains[0, next_block, 0:1, :]

            def norm_next(j):
                get_prior(j).wait()
                split_into(ahead, j, layer_norm(prior[j].astype(F32) + next_embed, next_gain).astype(BF16))
                for h in (0, 1):
                    for d in (2, 3, 1):
                        copy_f(h, j, d, True).start()

            over_rows(norm_next)
            for h in (0, 1):
                put_next(h).start()

    def moved(src, dst, send, recv, sending, h, d):
        peer = lax.rem(lat + d, n_lat)
        origin = lax.rem(lat - d + n_lat, n_lat)
        where = lat if sending else origin
        return pltpu.make_async_remote_copy(
            src_ref=src.at[h, peer], dst_ref=dst.at[h, where],
            send_sem=send.at[h, d], recv_sem=recv.at[h, d], device_id={"lat": peer}, device_id_type=MESH)

    def over_lat(step):
        def body(d, carry):
            step(d)
            return carry

        lax.fori_loop(1, n_lat, body, 0)

    def take_a(h, j):
        for d in (1, 2, 3):
            copy_a(h, j, d, False).wait_recv()

    def zonal(h, first, count):
        if handing:

            @pl.when(jnp.logical_not(first_section))
            def _():
                for j in range(first, first + count):
                    copy_e(h, j, 0).wait_recv()
                    take_a(h, j)
        else:
            for j in range(first, first + count):
                take_a(h, j)

        wide = jnp.concatenate(
            [x_all[h, :, j].reshape(4 * LON_PAD, half) for j in range(first, first + count)], axis=1)
        out = jnp.dot(fwd[...], wide, preferred_element_type=F32).astype(BF16)
        for i in range(count):
            spec[h, :, first + i] = out[:, i * half : (i + 1) * half].reshape(n_lat, MODE_PAD, half)

    for h in (0, 1):
        if handing:

            @pl.when(first_section)
            def _(h=h):
                get_next(h).wait()

        for first, count in ROWS:
            zonal(h, first, count)
        over_lat(lambda d, h=h: moved(spec, y_all, b_send, b_recv, True, h, d).start())

    rows = n_rows * MODE_PAD
    n_lines = n_lat * n_rows
    degree = lax.broadcasted_iota(jnp.int32, (n_degrees, half), 0)
    get_leg.wait()
    get_legt.wait()

    for h in (0, 1):

        def widen(src, value, h=h):
            at = pl.multiple_of(src * rows, 16)
            y_f32[h, pl.ds(at, rows), :] = value.reshape(rows, half).astype(F32)

        widen(lat, spec[h, lat])

        def take_b(d, h=h):
            moved(spec, y_all, b_send, b_recv, False, h, d).wait_recv()
            origin = lax.rem(lat - d + n_lat, n_lat)
            widen(origin, y_all[h, origin])

        over_lat(take_b)
        fil_re = filters[0, block, 0, :, h * half : (h + 1) * half]
        fil_im = filters[0, block, 1, :, h * half : (h + 1) * half]
        for m in range(m_local):
            pieces = [y_f32[h, pl.ds(r * m_local + m, n_lines, stride=MODE_PAD), :] for r in (0, 1)]
            column = jnp.concatenate(pieces, axis=1).astype(BF16)
            coeff = jnp.dot(leg[m], column, preferred_element_type=F32)
            co_re, co_im = coeff[:, :half], coeff[:, half:]
            order = lat * m_local + m
            keep = (degree < l_max) & (jnp.full((n_degrees, half), order, jnp.int32) < m_max)
            out_re = jnp.where(keep, co_re * fil_re - co_im * fil_im, 0.0)
            out_im = jnp.where(keep, co_re * fil_im + co_im * fil_re, 0.0)
            out = jnp.concatenate([out_re, out_im], axis=1).astype(BF16)
            lines = jnp.dot(legt[m], out, preferred_element_type=F32)
            for r in (0, 1):
                f_f32[h, pl.ds(r * m_local + m, n_lat * 8, stride=MODE_PAD), :] = lines[:, r * half : (r + 1) * half]

        def narrow(peer, h=h):
            at = pl.multiple_of(peer * (8 * MODE_PAD), 16)
            return f_f32[h, pl.ds(at, rows), :].astype(BF16).reshape(n_rows, MODE_PAD, half)

        def send_c(d, h=h):
            peer = lax.rem(lat + d, n_lat)
            back[h, peer] = narrow(peer)
            moved(back, z_all, c_send, c_recv, True, h, d).start()

        over_lat(send_c)
        z_all[h, lat] = narrow(lat)

    def copy_d(h, j, d, sending):
        peer = lon_peer(lon, d)
        slot = lon if sending else peer
        return pltpu.make_async_remote_copy(
            src_ref=o_all.at[h, peer, j], dst_ref=r_all.at[h, slot, j], send_sem=d_send.at[h, d, j],
            recv_sem=d_recv.at[h, d, j], device_id={"lon": peer}, device_id_type=MESH)

    for h in (0, 1):
        over_lat(lambda d, h=h: moved(back, z_all, c_send, c_recv, False, h, d).wait_recv())
        for first, count in ROWS:
            modes = jnp.concatenate(
                [z_all[h, :, j].reshape(n_lat * MODE_PAD, half) for j in range(first, first + count)], axis=1)
            out = jnp.dot(inv[...], modes, preferred_element_type=F32).astype(BF16)
            for i in range(count):
                j = first + i
                o_all[h, :, j] = out[:, i * half : (i + 1) * half].reshape(4, LON_PAD, half)
                for d in (2, 3, 1):
                    copy_d(h, j, d, True).start()
                r_all[h, lon, j] = o_all[h, lon, j]

    def put_v(j):
        return pltpu.make_async_copy(vbuf.at[j], v_out.at[j], loc.at[2 + j])

    def put_own(j):
        return pltpu.make_async_copy(nbuf.at[j], own_out.at[j], loc.at[2 + n_rows + j])

    def put_sib(j):
        return pltpu.make_async_remote_copy(
            src_ref=nbuf.at[j], dst_ref=sib_out.at[j], send_sem=n_send.at[j], recv_sem=n_recv.at[j],
            device_id={"lon": sibling}, device_id_type=MESH)

    if handing:

        @pl.when(jnp.logical_not(first_section))
        def _():
            over_rows(lambda j: copy_t(j).wait_recv())

        @pl.when(first_section)
        def _():
            over_rows(lambda j: get_tok(j).wait())

    def second_norm(j):
        for h in (0, 1):
            for d in (1, 2, 3):
                copy_d(h, j, d, False).wait_recv()
        spectral = jnp.concatenate(
            [r_all[h, q, j, 0:n_cols, :] for q in range(4) for h in (0, 1)], axis=1).astype(F32)
        mixed = tok[j].astype(F32) + embed + spectral
        vbuf[j] = mixed
        nbuf[j, 0:n_cols, :] = layer_norm(mixed, gain_two).astype(BF16)
        put_sib(j).start()
        put_v(j).start()
        put_own(j).start()

    over_rows(second_norm)

    def finish_a(j):
        for h in (0, 1):
            for d in (1, 2, 3):
                copy_a(h, j, d, True).wait_send()

    def finish_rows(j):
        for h in (0, 1):
            for d in (1, 2, 3):
                copy_d(h, j, d, True).wait_send()
        put_v(j).wait()
        put_own(j).wait()
        put_sib(j).wait()

    def finish_lat(d):
        for h in (0, 1):
            moved(spec, y_all, b_send, b_recv, True, h, d).wait_send()
            moved(back, z_all, c_send, c_recv, True, h, d).wait_send()

    if handing:

        def finish_handing(j):
            for h in (0, 1):
                for d in range(4):
                    copy_e(h, j, d).wait_send()
            copy_t(j).wait_send()

        @pl.when(first_section)
        def _():
            over_rows(finish_handing)
    else:

        def finish_next(j):
            for h in (0, 1):
                for d in (1, 2, 3):
                    copy_f(h, j, d, True).wait_send()
                    copy_f(h, j, d, False).wait_recv()

        @pl.when(first_section)
        def _():
            over_rows(finish_next)
            for h in (0, 1):
                put_next(h).wait()

        over_rows(finish_a)
    over_lat(finish_lat)
    over_rows(finish_rows)


def spectral_part(tick, n_section, plan, cutoff, lmax, mmax, tokens, cut_table, gains, filters, tables, prior=()):
    n_rows, n_cols, width = tokens.shape
    fwd, inv, leg, legt = tables
    n_lat, m_local, n_degrees, n_lines = leg.shape
    part = filters.shape[4]
    half = part // 2
    smem = pl.BlockSpec(memory_space=pltpu.SMEM)
    vmem = pl.BlockSpec(memory_space=pltpu.VMEM)
    anys = pl.BlockSpec(memory_space=pltpu.HBM)
    dma = pltpu.SemaphoreType.DMA
    lonwise = pltpu.VMEM((2, 4, n_rows, LON_PAD, half), BF16)
    latwise = pltpu.VMEM((2, n_lat, n_rows, MODE_PAD, half), BF16)
    small = pltpu.VMEM((16, 128), BF16)
    tokens_buf = pltpu.VMEM((n_rows, n_cols, width), BF16)
    return pl.pallas_call(
        functools.partial(spec_kernel, tick, n_section),
        out_shape=(
            jax.ShapeDtypeStruct((n_rows, n_cols, width), F32),
            jax.ShapeDtypeStruct((n_rows, LON_PAD, width), BF16),
            jax.ShapeDtypeStruct((n_rows, LON_PAD, width), BF16),
        ) + (() if tick else (jax.ShapeDtypeStruct(lonwise.shape, BF16),)),
        in_specs=[smem] * 4 + [anys] * 2 + ([vmem, anys] if tick else []) + [vmem] * 5 + [anys] * 2,
        out_specs=(anys,) * (3 if tick else 4),
        scratch_shapes=[
            tokens_buf, tokens_buf, small if tick else lonwise, lonwise, lonwise, latwise, latwise,
            pltpu.VMEM((2, n_lines * MODE_PAD, half), F32),
            pltpu.VMEM((2, n_lat * 8 * MODE_PAD, half), F32),
            latwise, latwise, lonwise, lonwise,
            pltpu.VMEM((n_rows, n_cols, width), F32),
            pltpu.VMEM((n_rows, LON_PAD, width), BF16),
            pltpu.VMEM(leg.shape[1:], BF16),
            pltpu.VMEM(legt.shape[1:], BF16),
            dma((2, 4, n_rows)), dma((2, 4, n_rows)), dma((2, 4, n_rows)), dma((2, 4, n_rows)),
            dma((n_rows,)), dma((n_rows,)),
            dma((2, n_lat)), dma((2, n_lat)),
            dma((2, n_lat)), dma((2, n_lat)),
            dma((2, 4, n_rows)), dma((2, 4, n_rows)),
            dma((n_rows,)), dma((n_rows,)),
            dma((2 + 2 * n_rows,)), dma((2, n_rows)), dma((2,)),
        ],
        compiler_params=pltpu.CompilerParams(
            collective_id=2 * tick, has_side_effects=True, vmem_limit_bytes=VMEM),
        cost_estimate=pl.CostEstimate(flops=5 * 10**10, bytes_accessed=10**7, transcendentals=0),
    )(plan, cutoff, lmax, mmax, tokens, *prior, cut_table, gains, filters, fwd, inv, leg, legt)


CHUNKS = 2
LATER = 2


def mlp_kernel(
    v_hbm, own_hbm, sib_hbm, w_hbm, out_hbm,
    x_all, wi, wo, acc, given, taken, vbuf, obuf, x_sem, w_sem, v_sem, o_sem, p_send, p_recv,
):
    lon = lax.axis_index("lon")
    sibling = lon_peer(lon, 1)
    n_rows, n_cols, width = v_hbm.shape
    ff = wi.shape[2]
    part = ff // CHUNKS
    shard = w_hbm.shape[1] // 2

    barrier = pltpu.get_barrier_semaphore()
    pl.semaphore_signal(barrier, inc=1, device_id={"lon": sibling}, device_id_type=MESH)

    get_x = [
        pltpu.make_async_copy(ref.at[pl.ds(first, count)], x_all.at[pl.ds(n_rows * k + first, count)], x_sem.at[2 * k + g])
        for k, ref in enumerate((sib_hbm, own_hbm))
        for g, (first, count) in enumerate(GROUPS)
    ]

    def get_wi(c):
        return pltpu.make_async_copy(w_hbm.at[:, pl.ds(0, shard), pl.ds(c * part, part)], wi.at[:, :, pl.ds(c * part, part)], w_sem.at[0, c])

    def get_wo(c):
        return pltpu.make_async_copy(w_hbm.at[:, pl.ds(shard, shard), pl.ds(c * part, part)], wo.at[:, :, pl.ds(c * part, part)], w_sem.at[1, c])

    get_v = pltpu.make_async_copy(v_hbm, vbuf, v_sem)
    get_x[0].start()
    for c in range(CHUNKS):
        get_wi(c).start()
        get_wo(c).start()
        if c == 0:
            get_x[1].start()
    get_x[2].start()
    get_x[3].start()
    get_v.start()
    pl.semaphore_wait(barrier, 1)

    def send(g):
        first, count = GROUPS[g]
        return pltpu.make_async_remote_copy(
            src_ref=given.at[pl.ds(first, count)], dst_ref=taken.at[pl.ds(first, count)],
            send_sem=p_send.at[g], recv_sem=p_recv.at[g], device_id={"lon": sibling}, device_id_type=MESH)

    def put(j):
        return pltpu.make_async_copy(obuf.at[j], out_hbm.at[j], o_sem.at[j])

    for tile in range(4):
        k, g = tile // 2, tile % 2
        first, count = GROUPS[g]
        size = count * LON_PAD
        get_x[tile].wait()

        x = x_all[pl.ds(n_rows * k + first, count)].reshape(size, width)
        pieces = CHUNKS if tile == 0 else LATER
        wide = ff // pieces
        for c in range(pieces):
            if tile == 0:
                get_wi(c).wait()
            at = c * wide
            before = jnp.dot(x, wi[:, :, at : at + wide].reshape(width, wide), preferred_element_type=F32)
            h = jax.nn.gelu(before).astype(BF16)
            if tile == 0:
                get_wo(c).wait()
            out = lax.dot_general(
                h, wo[:, :, at : at + wide].reshape(width, wide), (((1,), (1,)), ((), ())), preferred_element_type=F32)
            acc[0:size, :] = out if c == 0 else acc[0:size, :] + out
        total = acc[0:size, :].reshape(count, LON_PAD, width)
        if k == 0:
            given[pl.ds(first, count)] = total.astype(BF16)
            send(g).start()
        else:
            if g == 0:
                get_v.wait()
            send(g).wait_recv()
            for i in range(count):
                j = first + i
                other = taken[j, 0:n_cols, :].astype(F32)
                obuf[j] = (vbuf[j] + (total[i, 0:n_cols, :] + other)).astype(BF16)
                put(j).start()
    for j in range(n_rows):
        put(j).wait()
    for g in range(2):
        send(g).wait_send()


def mlp_part(tick, v, own, sib, weights):
    n_rows, n_cols, width = v.shape
    n_lat, shard, ff = weights.shape
    shard = shard // 2
    anys = pl.BlockSpec(memory_space=pltpu.HBM)
    dma = pltpu.SemaphoreType.DMA
    most = max(count for _, count in GROUPS)
    return pl.pallas_call(
        mlp_kernel,
        out_shape=jax.ShapeDtypeStruct((n_rows, n_cols, width), BF16),
        in_specs=[anys] * 4,
        out_specs=anys,
        scratch_shapes=[
            pltpu.VMEM((2 * n_rows, LON_PAD, width), BF16),
            pltpu.VMEM((n_lat, shard, ff), BF16),
            pltpu.VMEM((n_lat, shard, ff), BF16),
            pltpu.VMEM((most * LON_PAD, width), F32),
            pltpu.VMEM((n_rows, LON_PAD, width), BF16),
            pltpu.VMEM((n_rows, LON_PAD, width), BF16),
            pltpu.VMEM((n_rows, n_cols, width), F32),
            pltpu.VMEM((n_rows, n_cols, width), BF16),
            dma((4,)), dma((2, CHUNKS)), dma(()), dma((n_rows,)), dma((2,)), dma((2,)),
        ],
        compiler_params=pltpu.CompilerParams(
            collective_id=2 * tick + 1, has_side_effects=True, vmem_limit_bytes=VMEM),
        cost_estimate=pl.CostEstimate(flops=10**10, bytes_accessed=10**7, transcendentals=0),
    )(v, own, sib, weights)


def pick_kernel(plan, w_in, w_out, first, second, sem):
    section = lax.axis_index("section")
    core = lax.rem(lax.axis_index("lon"), 2)
    shard, ff = w_in.shape[2], w_in.shape[3] // 2
    columns = pl.ds(pl.multiple_of(core * ff, ff), ff)
    copies = [
        pltpu.make_async_copy(ref.at[0, plan[tick, section], :, columns], out.at[pl.ds(k * shard, shard)], sem.at[tick, k])
        for tick, out in enumerate((first, second))
        for k, ref in enumerate((w_in, w_out))
    ]
    for copy in copies:
        copy.start()
    for copy in copies:
        copy.wait()


def own_weights(plan, w_in, w_out):
    anys = pl.BlockSpec(memory_space=pltpu.HBM)
    out = jax.ShapeDtypeStruct((2 * w_in.shape[2], w_in.shape[3] // 2), BF16)
    return pl.pallas_call(
        pick_kernel,
        out_shape=(out, out),
        in_specs=[pl.BlockSpec(memory_space=pltpu.SMEM), anys, anys],
        out_specs=(pl.BlockSpec(memory_space=pltpu.VMEM),) * 2,
        scratch_shapes=[pltpu.SemaphoreType.DMA((2, 2))],
        compiler_params=pltpu.CompilerParams(vmem_limit_bytes=VMEM),
    )(plan, w_in, w_out)


def local(state, fresh, cutoff, plan, lmax, mmax, cutoff_table, norm_gains, filters, w_in, w_out):
    n_section = lax.axis_size("section")
    n_lat = lax.axis_size("lat")
    n_lon = lax.axis_size("lon")
    n_rows, n_cols, width = fresh.shape
    n_degrees = filters.shape[3]
    tables = [jnp.asarray(t) for t in spectral_tables(n_lat, n_lon, n_rows, n_cols, n_degrees)]
    weights = [lax.all_gather(mine, "lat", axis=0) for mine in own_weights(plan, w_in, w_out)]
    other_gains = passed_along(norm_gains, "section", -1)

    def spectral(tick, tokens, *more):
        return spectral_part(
            tick, n_section, plan, cutoff, lmax, mmax, tokens, cutoff_table, norm_gains, filters, tables, more)

    *parts, entering = spectral(0, state[0], fresh)
    first_out = mlp_part(0, *parts, weights[0])
    parts = spectral(1, fresh, first_out, other_gains, entering)
    second_out = mlp_part(1, *parts, weights[1])
    return (first_out[None], second_out[None])


def solution(mesh):
    return jax.shard_map(
        local,
        mesh=mesh,
        in_specs=(
            P("section", "lat", "lon", None),
            P("lat", "lon", None),
            P(),
            P(),
            P(),
            P(),
            P(),
            P("section", None, None, None),
            P("section", None, None, None, "lon"),
            P("section", None, "lat", None),
            P("section", None, "lat", None),
        ),
        out_specs=(P("section", "lat", "lon", None), P("section", "lat", "lon", None)),
        check_vma=False,
    )
```

```python
import functools
import math

import jax
import jax.numpy as jnp
import numpy as np
from jax import lax
from jax.experimental import pallas as pl
from jax.experimental.pallas import tpu as pltpu
from jax.sharding import PartitionSpec as P

MM = 96
MESH = pl.DeviceIdType.MESH
BF16 = jnp.bfloat16
F32 = jnp.float32
VMEM = 60 * 1024 * 1024
LON_PAD = 96
MODE_PAD = 16
GROUPS = ((0, 4), (4, 3))
ROWS = ((0, 2), (2, 2), (4, 3))


def passed_along(value, axis, steps):
    count = lax.axis_size(axis)
    leading, last = (max(0, -steps), min(count, count - steps))
    return lax.ppermute(value, axis, [(source, source + steps) for source in range(leading, last)])


def legendre_table(n_orders, n_rows, n_degrees):
    theta = math.pi * (np.arange(n_rows) + 0.5) / n_rows
    cosine, sine = np.cos(theta), np.sin(theta)
    table = np.zeros((n_degrees, n_orders, n_rows))
    for m in range(n_orders):
        log_start = (
            0.5 * math.log((2.0 * m + 1.0) / (4.0 * math.pi))
            + math.lgamma(m + 0.5) - math.lgamma(0.5) - math.lgamma(m + 1.0)
        )
        table[m, m] = np.exp(log_start + m * np.log(sine))
        for l in range(m + 1, n_degrees):
            coef_a = math.sqrt((4.0 * l * l - 1.0) / (l * l - m * m))
            coef_b = math.sqrt(max((l - 1.0) ** 2 - m * m, 0.0) / max(4.0 * (l - 1.0) ** 2 - 1.0, 1.0))
            before = table[l - 2, m] if l - 2 >= m else 0.0
            table[l, m] = coef_a * (cosine * table[l - 1, m] - coef_b * before)
    quad = 2.0 * math.pi * (math.pi / n_rows) * sine
    return table, table * quad


def spectral_tables(n_lat, n_lon, n_rows, n_cols, n_degrees):
    m_local = MM // n_lat
    all_cols = n_cols * n_lon
    phase = 2.0 * math.pi * ((np.arange(all_cols)[:, None] * np.arange(MM)[None, :]) % all_cols) / all_cols
    weight = np.where(np.arange(MM) == 0, 1.0, 2.0)
    forward = np.zeros((n_lat, MODE_PAD, n_lon, LON_PAD))
    inverse = np.zeros((n_lon, LON_PAD, n_lat, MODE_PAD))
    parts = ((np.cos(phase) / all_cols, weight * np.cos(phase)), (-np.sin(phase) / all_cols, -weight * np.sin(phase)))
    for r, (fwd, inv) in enumerate(parts):
        fwd = fwd.reshape(n_lon, n_cols, n_lat, m_local)
        inv = inv.reshape(n_lon, n_cols, n_lat, m_local)
        forward[:, r * m_local : (r + 1) * m_local, :, :n_cols] = fwd.transpose(2, 3, 0, 1)
        inverse[:, :n_cols, :, r * m_local : (r + 1) * m_local] = inv
    forward = forward.reshape(n_lat * MODE_PAD, n_lon * LON_PAD)
    inverse = inverse.reshape(n_lon * LON_PAD, n_lat * MODE_PAD)
    plain, weighted = legendre_table(MM, n_rows * n_lat, n_degrees)
    split = (n_degrees, n_lat, m_local, n_lat, n_rows)
    weighted = weighted.reshape(split).transpose(1, 2, 0, 3, 4).reshape(n_lat, m_local, n_degrees, n_lat * n_rows)
    padded = np.zeros((n_lat, m_local, n_lat, 8, n_degrees))
    padded[:, :, :, :n_rows] = plain.reshape(split).transpose(1, 2, 3, 4, 0)
    padded = padded.reshape(n_lat, m_local, n_lat * 8, n_degrees)
    return tuple(t.astype(BF16) for t in (forward, inverse, weighted, padded))


def normed_parts(values):
    scale = 1.0 / values.shape[-1]
    mean = jnp.sum(values, axis=-1, keepdims=True) * scale
    center = values - mean
    spread = jnp.sum(center * center, axis=-1, keepdims=True) * scale
    return center, mean, lax.rsqrt(spread + 1e-05)


def layer_norm(values, gain):
    center, _, scale = normed_parts(values)
    return center * scale * gain


def lon_peer(me, d):
    return lax.rem(me // 2 + d // 2, 2) * 2 + lax.rem(lax.rem(me, 2) + d % 2, 2)


def spec_kernel(
    tick, n_section, plan, cutoff, lmax, mmax, *refs,
):
    if tick == 0:
        tok_hbm, prior_hbm, *refs = refs
    else:
        tok_hbm, prior_hbm, other_gains, x_next, *refs = refs
    cut_table, gains, filters, fwd, inv, leg_hbm, legt_hbm, v_out, own_out, sib_out, *refs = refs
    if tick == 0:
        x_next, *refs = refs
    (
        tok, prior, norm, ahead, x_all, spec, y_all, y_f32, f_f32, back, z_all, o_all, r_all, vbuf, nbuf, leg, legt,
        a_send, a_recv, e_send, f_recv, t_send, t_recv, b_send, b_recv, c_send, c_recv, d_send, d_recv, n_send, n_recv, loc, row_in, next_sem,
        stat, stat_all, raw_in, stat_send, stat_recv, raw_send, raw_recv,
    ) = refs
    section, lat, lon = (lax.axis_index(a) for a in ("section", "lat", "lon"))
    n_lat = spec.shape[1]
    n_rows, n_cols, width = tok.shape
    n_degrees, part = filters.shape[3], filters.shape[4]
    m_local = leg.shape[0]
    half = part // 2
    sibling = lon_peer(lon, 1)
    handing = tick > 0
    first_section = section == 0

    barrier = pltpu.get_barrier_semaphore()
    greeted = 3 + n_lat - 1
    for d in (1, 2, 3):
        pl.semaphore_signal(barrier, inc=1, device_id={"lon": lon_peer(lon, d)}, device_id_type=MESH)
    if handing:
        greeted += 4
        for q in range(4):
            pl.semaphore_signal(barrier, inc=1, device_id={"section": 1 - section, "lon": q}, device_id_type=MESH)

    def greet(d, carry):
        pl.semaphore_signal(barrier, inc=1, device_id={"lat": lax.rem(lat + d, n_lat)}, device_id_type=MESH)
        return carry

    lax.fori_loop(1, n_lat, greet, 0)

    def get_tok(j):
        return pltpu.make_async_copy(tok_hbm.at[j], tok.at[j], row_in.at[0, j])

    def get_prior(j):
        return pltpu.make_async_copy(prior_hbm.at[j], prior.at[j], row_in.at[1, j])

    def get_next(h):
        return pltpu.make_async_copy(x_next.at[h], x_all.at[h], next_sem.at[h])

    def put_next(h):
        return pltpu.make_async_copy(ahead.at[h, lon], x_next.at[h, lon], next_sem.at[h])

    def over_rows(step):
        def body(j, carry):
            step(j)
            return carry

        lax.fori_loop(0, n_rows, body, 0)

    if handing:

        @pl.when(first_section)
        def _():
            over_rows(lambda j: get_prior(j).start())
            for h in (0, 1):
                get_next(h).start()
            over_rows(lambda j: get_tok(j).start())
    else:
        over_rows(lambda j: get_tok(j).start())

        @pl.when(first_section)
        def _():
            over_rows(lambda j: get_prior(j).start())
    get_leg = pltpu.make_async_copy(leg_hbm.at[lat], leg, loc.at[0])
    get_legt = pltpu.make_async_copy(legt_hbm.at[lat], legt, loc.at[1])
    get_leg.start()
    get_legt.start()

    block = plan[tick, section]
    cut = cutoff[tick - section + n_section - 1]
    l_max, m_max = lmax[section], mmax[section]
    embed = cut_table[pl.ds(cut, 1), :]
    gain_one = gains[0, block, 0:1, :]
    gain_two = gains[0, block, 1:2, :]
    pad = jnp.zeros((2, 4, n_rows, 16, half), BF16)
    ahead[:, :, :, LON_PAD - 16 :, :] = pad
    if not handing:
        norm[:, :, :, LON_PAD - 16 :, :] = pad
    f_f32[...] = jnp.zeros_like(f_f32)
    nbuf[:, LON_PAD - 16 :, :] = jnp.zeros((n_rows, 16, width), BF16)
    pl.semaphore_wait(barrier, greeted)

    def copy_a(h, j, d, sending):
        peer = lon_peer(lon, d)
        slot = lon if sending else peer
        return pltpu.make_async_remote_copy(
            src_ref=norm.at[h, peer, j] if sending else x_all.at[h, slot, j], dst_ref=x_all.at[h, slot, j], send_sem=a_send.at[h, d, j],
            recv_sem=a_recv.at[h, d, j], device_id={"lon": peer}, device_id_type=MESH)

    def copy_e(h, j, d):
        peer = lon_peer(lon, d)
        return pltpu.make_async_remote_copy(
            src_ref=ahead.at[h, peer, j], dst_ref=x_all.at[h, lon, j], send_sem=e_send.at[h, d, j],
            recv_sem=a_recv.at[h, d, j], device_id={"section": 1 - section, "lon": peer}, device_id_type=MESH)

    def copy_f(h, j, d, sending):
        peer = lon_peer(lon, d)
        slot = lon if sending else peer
        return pltpu.make_async_remote_copy(
            src_ref=ahead.at[h, peer, j], dst_ref=x_next.at[h, slot, j], send_sem=e_send.at[h, d, j],
            recv_sem=f_recv.at[h, d, j], device_id={"lon": peer}, device_id_type=MESH)

    chip = lon // 2
    far = pl.ds(pl.multiple_of((1 - chip) * 2 * part, part), 2 * part)

    def copy_t(j):
        return pltpu.make_async_remote_copy(
            src_ref=prior.at[j, :, far], dst_ref=tok.at[j, :, far], send_sem=t_send.at[j], recv_sem=t_recv.at[j],
            device_id={"section": 1 - section}, device_id_type=MESH)

    def copy_stat(d, sending):
        peer = lon_peer(lon, d)
        slot = lon if sending else peer
        return pltpu.make_async_remote_copy(
            src_ref=stat, dst_ref=stat_all.at[slot], send_sem=stat_send.at[d], recv_sem=stat_recv.at[d],
            device_id={"section": 1 - section, "lon": peer}, device_id_type=MESH)

    def copy_raw(h):
        return pltpu.make_async_remote_copy(
            src_ref=x_all.at[h, sibling], dst_ref=raw_in.at[h], send_sem=raw_send.at[h], recv_sem=raw_recv.at[h],
            device_id={"lon": sibling}, device_id_type=MESH)

    def split_into(dst, j, out):
        for q in range(4):
            for h in (0, 1):
                at = q * part + h * half
                dst[h, q, j, 0:n_cols, :] = out[:, at : at + half]

    def first_norm(j):
        get_tok(j).wait()
        split_into(norm, j, layer_norm(tok[j].astype(F32) + embed, gain_one).astype(BF16))
        for d in (2, 3, 1):
            copy_a(0, j, d, True).start()
        for h in (0, 1):
            x_all[h, lon, j] = norm[h, lon, j]

    def first_norm_rest(j):
        for d in (2, 3, 1):
            copy_a(1, j, d, True).start()

    if handing:

        @pl.when(first_section)
        def _():
            next_block = plan[tick, 1]
            next_embed = cut_table[pl.ds(cutoff[tick - 1 + n_section - 1], 1), :]
            next_gain = other_gains[0, next_block, 0:1, :]

            stat[...] = jnp.zeros_like(stat)
            lane = lax.broadcasted_iota(jnp.int32, (n_cols, stat.shape[1]), 1)

            def norm_ahead(j):
                get_prior(j).wait()
                raw = prior[j].astype(F32)
                center, mean, scale = normed_parts(raw + next_embed)
                out = center * scale * next_gain
                for q in range(4):
                    at = slice(q * part, (q + 1) * part)
                    mixed = jnp.where(chip == q // 2, raw[:, at], out[:, at]).astype(BF16)
                    for h in (0, 1):
                        ahead[h, q, j, 0:n_cols, :] = mixed[:, h * half : (h + 1) * half]
                for d in range(4):
                    copy_e(0, j, d).start()
                old = stat[0:n_cols, :]
                stat[0:n_cols, :] = jnp.where(lane == 2 * j, mean, jnp.where(lane == 2 * j + 1, scale, old))

            def norm_ahead_rest(j):
                for d in range(4):
                    copy_e(1, j, d).start()

            over_rows(norm_ahead)
            for d in (0, 1):
                copy_stat(d, True).start()
            over_rows(norm_ahead_rest)
            over_rows(lambda j: copy_t(j).start())
    else:
        over_rows(first_norm)
        over_rows(first_norm_rest)

        @pl.when(first_section)
        def _():
            next_block = plan[tick + 1, 0]
            next_embed = cut_table[pl.ds(cutoff[tick + 1 + n_section - 1], 1), :]
            next_gain = gains[0, next_block, 0:1, :]

            def norm_next(j):
                get_prior(j).wait()
                split_into(ahead, j, layer_norm(prior[j].astype(F32) + next_embed, next_gain).astype(BF16))
                for h in (0, 1):
                    for d in (2, 3, 1):
                        copy_f(h, j, d, True).start()

            over_rows(norm_next)
            for h in (0, 1):
                put_next(h).start()

    def moved(src, dst, send, recv, sending, h, d):
        peer = lax.rem(lat + d, n_lat)
        origin = lax.rem(lat - d + n_lat, n_lat)
        where = lat if sending else origin
        return pltpu.make_async_remote_copy(
            src_ref=src.at[h, peer], dst_ref=dst.at[h, where],
            send_sem=send.at[h, d], recv_sem=recv.at[h, d], device_id={"lat": peer}, device_id_type=MESH)

    def over_lat(step):
        def body(d, carry):
            step(d)
            return carry

        lax.fori_loop(1, n_lat, body, 0)

    def take_a(h, j):
        for d in (1, 2, 3):
            copy_a(h, j, d, False).wait_recv()

    def of_lon(row, h):
        out = row[:, h * half : (h + 1) * half]
        for q in (1, 2, 3):
            out = jnp.where(lon == q, row[:, q * part + h * half : q * part + (h + 1) * half], out)
        return out

    def arrived(h, j):
        if not handing:
            return x_all[h, :, j].reshape(4 * LON_PAD, half)
        shift, gain = of_lon(embed, h), of_lon(gain_one, h)
        rows_of = []
        for q in range(4):
            raw = x_all[h, q, j].astype(F32)
            out = (raw + shift - stat_all[q, :, 2 * j : 2 * j + 1]) * stat_all[q, :, 2 * j + 1 : 2 * j + 2] * gain
            is_raw = jnp.logical_and(section > 0, chip == q // 2)
            rows_of.append(jnp.where(is_raw, out, raw).astype(BF16))
        return jnp.concatenate(rows_of, axis=0)

    def zonal(h, first, count):
        if handing:

            @pl.when(jnp.logical_not(first_section))
            def _():
                for j in range(first, first + count):
                    copy_e(h, j, 0).wait_recv()
                    take_a(h, j)
        else:
            for j in range(first, first + count):
                take_a(h, j)

        wide = jnp.concatenate([arrived(h, j) for j in range(first, first + count)], axis=1)
        out = jnp.dot(fwd[...], wide, preferred_element_type=F32).astype(BF16)
        for i in range(count):
            spec[h, :, first + i] = out[:, i * half : (i + 1) * half].reshape(n_lat, MODE_PAD, half)

    for h in (0, 1):
        if handing:

            @pl.when(first_section)
            def _(h=h):
                get_next(h).wait()

            if h == 0:

                @pl.when(jnp.logical_not(first_section))
                def _():
                    for d in (0, 1):
                        copy_stat(d, False).wait_recv()

        for first, count in ROWS:
            zonal(h, first, count)
        if handing:

            @pl.when(jnp.logical_not(first_section))
            def _(h=h):
                copy_raw(h).start()

        over_lat(lambda d, h=h: moved(spec, y_all, b_send, b_recv, True, h, d).start())

    rows = n_rows * MODE_PAD
    n_lines = n_lat * n_rows
    degree = lax.broadcasted_iota(jnp.int32, (n_degrees, half), 0)
    get_leg.wait()
    get_legt.wait()

    for h in (0, 1):

        def widen(src, value, h=h):
            at = pl.multiple_of(src * rows, 16)
            y_f32[h, pl.ds(at, rows), :] = value.reshape(rows, half).astype(F32)

        widen(lat, spec[h, lat])

        def take_b(d, h=h):
            moved(spec, y_all, b_send, b_recv, False, h, d).wait_recv()
            origin = lax.rem(lat - d + n_lat, n_lat)
            widen(origin, y_all[h, origin])

        over_lat(take_b)
        fil_re = filters[0, block, 0, :, h * half : (h + 1) * half]
        fil_im = filters[0, block, 1, :, h * half : (h + 1) * half]
        for m in range(m_local):
            pieces = [y_f32[h, pl.ds(r * m_local + m, n_lines, stride=MODE_PAD), :] for r in (0, 1)]
            column = jnp.concatenate(pieces, axis=1).astype(BF16)
            coeff = jnp.dot(leg[m], column, preferred_element_type=F32)
            co_re, co_im = coeff[:, :half], coeff[:, half:]
            order = lat * m_local + m
            keep = (degree < l_max) & (jnp.full((n_degrees, half), order, jnp.int32) < m_max)
            out_re = jnp.where(keep, co_re * fil_re - co_im * fil_im, 0.0)
            out_im = jnp.where(keep, co_re * fil_im + co_im * fil_re, 0.0)
            out = jnp.concatenate([out_re, out_im], axis=1).astype(BF16)
            lines = jnp.dot(legt[m], out, preferred_element_type=F32)
            for r in (0, 1):
                f_f32[h, pl.ds(r * m_local + m, n_lat * 8, stride=MODE_PAD), :] = lines[:, r * half : (r + 1) * half]

        def narrow(peer, h=h):
            at = pl.multiple_of(peer * (8 * MODE_PAD), 16)
            return f_f32[h, pl.ds(at, rows), :].astype(BF16).reshape(n_rows, MODE_PAD, half)

        def send_c(d, h=h):
            peer = lax.rem(lat + d, n_lat)
            back[h, peer] = narrow(peer)
            moved(back, z_all, c_send, c_recv, True, h, d).start()

        over_lat(send_c)
        z_all[h, lat] = narrow(lat)

    def copy_d(h, j, d, sending):
        peer = lon_peer(lon, d)
        slot = lon if sending else peer
        return pltpu.make_async_remote_copy(
            src_ref=o_all.at[h, peer, j], dst_ref=r_all.at[h, slot, j], send_sem=d_send.at[h, d, j],
            recv_sem=d_recv.at[h, d, j], device_id={"lon": peer}, device_id_type=MESH)

    for h in (0, 1):
        over_lat(lambda d, h=h: moved(back, z_all, c_send, c_recv, False, h, d).wait_recv())
        for first, count in ROWS:
            modes = jnp.concatenate(
                [z_all[h, :, j].reshape(n_lat * MODE_PAD, half) for j in range(first, first + count)], axis=1)
            out = jnp.dot(inv[...], modes, preferred_element_type=F32).astype(BF16)
            for i in range(count):
                j = first + i
                o_all[h, :, j] = out[:, i * half : (i + 1) * half].reshape(4, LON_PAD, half)
                for d in (2, 3, 1):
                    copy_d(h, j, d, True).start()
                r_all[h, lon, j] = o_all[h, lon, j]

    def put_v(j):
        return pltpu.make_async_copy(vbuf.at[j], v_out.at[j], loc.at[2 + j])

    def put_own(j):
        return pltpu.make_async_copy(nbuf.at[j], own_out.at[j], loc.at[2 + n_rows + j])

    def put_sib(j):
        return pltpu.make_async_remote_copy(
            src_ref=nbuf.at[j], dst_ref=sib_out.at[j], send_sem=n_send.at[j], recv_sem=n_recv.at[j],
            device_id={"lon": sibling}, device_id_type=MESH)

    if handing:

        @pl.when(jnp.logical_not(first_section))
        def _():
            for h in (0, 1):
                copy_raw(h).wait_recv()

            def assemble(j):
                copy_t(j).wait_recv()
                for h in (0, 1):
                    mine = pl.ds(pl.multiple_of(lon * part + h * half, half), half)
                    other = pl.ds(pl.multiple_of(sibling * part + h * half, half), half)
                    tok[j, :, mine] = x_all[h, lon, j, 0:n_cols, :]
                    tok[j, :, other] = raw_in[h, j, 0:n_cols, :]

            over_rows(assemble)

        @pl.when(first_section)
        def _():
            over_rows(lambda j: get_tok(j).wait())

    def second_norm(j):
        for h in (0, 1):
            for d in (1, 2, 3):
                copy_d(h, j, d, False).wait_recv()
        spectral = jnp.concatenate(
            [r_all[h, q, j, 0:n_cols, :] for q in range(4) for h in (0, 1)], axis=1).astype(F32)
        mixed = tok[j].astype(F32) + embed + spectral
        vbuf[j] = mixed
        nbuf[j, 0:n_cols, :] = layer_norm(mixed, gain_two).astype(BF16)
        put_sib(j).start()
        put_v(j).start()
        put_own(j).start()

    over_rows(second_norm)

    def finish_a(j):
        for h in (0, 1):
            for d in (1, 2, 3):
                copy_a(h, j, d, True).wait_send()

    def finish_rows(j):
        for h in (0, 1):
            for d in (1, 2, 3):
                copy_d(h, j, d, True).wait_send()
        put_v(j).wait()
        put_own(j).wait()
        put_sib(j).wait()

    def finish_lat(d):
        for h in (0, 1):
            moved(spec, y_all, b_send, b_recv, True, h, d).wait_send()
            moved(back, z_all, c_send, c_recv, True, h, d).wait_send()

    if handing:

        def finish_handing(j):
            for h in (0, 1):
                for d in range(4):
                    copy_e(h, j, d).wait_send()
            copy_t(j).wait_send()

        @pl.when(first_section)
        def _():
            over_rows(finish_handing)
            for d in (0, 1):
                copy_stat(d, True).wait_send()

        @pl.when(jnp.logical_not(first_section))
        def _():
            for h in (0, 1):
                copy_raw(h).wait_send()
    else:

        def finish_next(j):
            for h in (0, 1):
                for d in (1, 2, 3):
                    copy_f(h, j, d, True).wait_send()
                    copy_f(h, j, d, False).wait_recv()

        @pl.when(first_section)
        def _():
            over_rows(finish_next)
            for h in (0, 1):
                put_next(h).wait()

        over_rows(finish_a)
    over_lat(finish_lat)
    over_rows(finish_rows)


def spectral_part(tick, n_section, plan, cutoff, lmax, mmax, tokens, cut_table, gains, filters, tables, prior=()):
    n_rows, n_cols, width = tokens.shape
    fwd, inv, leg, legt = tables
    n_lat, m_local, n_degrees, n_lines = leg.shape
    part = filters.shape[4]
    half = part // 2
    smem = pl.BlockSpec(memory_space=pltpu.SMEM)
    vmem = pl.BlockSpec(memory_space=pltpu.VMEM)
    anys = pl.BlockSpec(memory_space=pltpu.HBM)
    dma = pltpu.SemaphoreType.DMA
    lonwise = pltpu.VMEM((2, 4, n_rows, LON_PAD, half), BF16)
    latwise = pltpu.VMEM((2, n_lat, n_rows, MODE_PAD, half), BF16)
    small = pltpu.VMEM((16, 128), BF16)
    tokens_buf = pltpu.VMEM((n_rows, n_cols, width), BF16)
    return pl.pallas_call(
        functools.partial(spec_kernel, tick, n_section),
        out_shape=(
            jax.ShapeDtypeStruct((n_rows, n_cols, width), F32),
            jax.ShapeDtypeStruct((n_rows, LON_PAD, width), BF16),
            jax.ShapeDtypeStruct((n_rows, LON_PAD, width), BF16),
        ) + (() if tick else (jax.ShapeDtypeStruct(lonwise.shape, BF16),)),
        in_specs=[smem] * 4 + [anys] * 2 + ([vmem, anys] if tick else []) + [vmem] * 5 + [anys] * 2,
        out_specs=(anys,) * (3 if tick else 4),
        scratch_shapes=[
            tokens_buf, tokens_buf, small if tick else lonwise, lonwise, lonwise, latwise, latwise,
            pltpu.VMEM((2, n_lines * MODE_PAD, half), F32),
            pltpu.VMEM((2, n_lat * 8 * MODE_PAD, half), F32),
            latwise, latwise, lonwise, lonwise,
            pltpu.VMEM((n_rows, n_cols, width), F32),
            pltpu.VMEM((n_rows, LON_PAD, width), BF16),
            pltpu.VMEM(leg.shape[1:], BF16),
            pltpu.VMEM(legt.shape[1:], BF16),
            dma((2, 4, n_rows)), dma((2, 4, n_rows)), dma((2, 4, n_rows)), dma((2, 4, n_rows)),
            dma((n_rows,)), dma((n_rows,)),
            dma((2, n_lat)), dma((2, n_lat)),
            dma((2, n_lat)), dma((2, n_lat)),
            dma((2, 4, n_rows)), dma((2, 4, n_rows)),
            dma((n_rows,)), dma((n_rows,)),
            dma((2 + 2 * n_rows,)), dma((2, n_rows)), dma((2,)),
            pltpu.VMEM((LON_PAD, 128), F32),
            pltpu.VMEM((4, LON_PAD, 128), F32),
            pltpu.VMEM((2, n_rows, LON_PAD, half), BF16) if tick else small,
            dma((2,)), dma((2,)), dma((2,)), dma((2,)),
        ],
        compiler_params=pltpu.CompilerParams(
            collective_id=2 * tick, has_side_effects=True, vmem_limit_bytes=VMEM),
        cost_estimate=pl.CostEstimate(flops=5 * 10**10, bytes_accessed=10**7, transcendentals=0),
    )(plan, cutoff, lmax, mmax, tokens, *prior, cut_table, gains, filters, fwd, inv, leg, legt)


CHUNKS = 2
LATER = 2


def mlp_kernel(
    v_hbm, own_hbm, sib_hbm, w_hbm, out_hbm,
    x_all, wi, wo, acc, given, taken, vbuf, obuf, x_sem, w_sem, v_sem, o_sem, p_send, p_recv,
):
    lon = lax.axis_index("lon")
    sibling = lon_peer(lon, 1)
    n_rows, n_cols, width = v_hbm.shape
    ff = wi.shape[2]
    part = ff // CHUNKS
    shard = w_hbm.shape[1] // 2

    barrier = pltpu.get_barrier_semaphore()
    pl.semaphore_signal(barrier, inc=1, device_id={"lon": sibling}, device_id_type=MESH)

    get_x = [
        pltpu.make_async_copy(ref.at[pl.ds(first, count)], x_all.at[pl.ds(n_rows * k + first, count)], x_sem.at[2 * k + g])
        for k, ref in enumerate((sib_hbm, own_hbm))
        for g, (first, count) in enumerate(GROUPS)
    ]

    def get_wi(c):
        return pltpu.make_async_copy(w_hbm.at[:, pl.ds(0, shard), pl.ds(c * part, part)], wi.at[:, :, pl.ds(c * part, part)], w_sem.at[0, c])

    def get_wo(c):
        return pltpu.make_async_copy(w_hbm.at[:, pl.ds(shard, shard), pl.ds(c * part, part)], wo.at[:, :, pl.ds(c * part, part)], w_sem.at[1, c])

    get_v = pltpu.make_async_copy(v_hbm, vbuf, v_sem)
    get_x[0].start()
    for c in range(CHUNKS):
        get_wi(c).start()
        get_wo(c).start()
        if c == 0:
            get_x[1].start()
    get_x[2].start()
    get_x[3].start()
    get_v.start()
    pl.semaphore_wait(barrier, 1)

    def send(g):
        first, count = GROUPS[g]
        return pltpu.make_async_remote_copy(
            src_ref=given.at[pl.ds(first, count)], dst_ref=taken.at[pl.ds(first, count)],
            send_sem=p_send.at[g], recv_sem=p_recv.at[g], device_id={"lon": sibling}, device_id_type=MESH)

    def put(j):
        return pltpu.make_async_copy(obuf.at[j], out_hbm.at[j], o_sem.at[j])

    for tile in range(4):
        k, g = tile // 2, tile % 2
        first, count = GROUPS[g]
        size = count * LON_PAD
        get_x[tile].wait()

        x = x_all[pl.ds(n_rows * k + first, count)].reshape(size, width)
        pieces = CHUNKS if tile == 0 else LATER
        wide = ff // pieces
        for c in range(pieces):
            if tile == 0:
                get_wi(c).wait()
            at = c * wide
            before = jnp.dot(x, wi[:, :, at : at + wide].reshape(width, wide), preferred_element_type=F32)
            h = jax.nn.gelu(before).astype(BF16)
            if tile == 0:
                get_wo(c).wait()
            out = lax.dot_general(
                h, wo[:, :, at : at + wide].reshape(width, wide), (((1,), (1,)), ((), ())), preferred_element_type=F32)
            acc[0:size, :] = out if c == 0 else acc[0:size, :] + out
        total = acc[0:size, :].reshape(count, LON_PAD, width)
        if k == 0:
            given[pl.ds(first, count)] = total.astype(BF16)
            send(g).start()
        else:
            if g == 0:
                get_v.wait()
            send(g).wait_recv()
            for i in range(count):
                j = first + i
                other = taken[j, 0:n_cols, :].astype(F32)
                obuf[j] = (vbuf[j] + (total[i, 0:n_cols, :] + other)).astype(BF16)
                put(j).start()
    for j in range(n_rows):
        put(j).wait()
    for g in range(2):
        send(g).wait_send()


def mlp_part(tick, v, own, sib, weights):
    n_rows, n_cols, width = v.shape
    n_lat, shard, ff = weights.shape
    shard = shard // 2
    anys = pl.BlockSpec(memory_space=pltpu.HBM)
    dma = pltpu.SemaphoreType.DMA
    most = max(count for _, count in GROUPS)
    return pl.pallas_call(
        mlp_kernel,
        out_shape=jax.ShapeDtypeStruct((n_rows, n_cols, width), BF16),
        in_specs=[anys] * 4,
        out_specs=anys,
        scratch_shapes=[
            pltpu.VMEM((2 * n_rows, LON_PAD, width), BF16),
            pltpu.VMEM((n_lat, shard, ff), BF16),
            pltpu.VMEM((n_lat, shard, ff), BF16),
            pltpu.VMEM((most * LON_PAD, width), F32),
            pltpu.VMEM((n_rows, LON_PAD, width), BF16),
            pltpu.VMEM((n_rows, LON_PAD, width), BF16),
            pltpu.VMEM((n_rows, n_cols, width), F32),
            pltpu.VMEM((n_rows, n_cols, width), BF16),
            dma((4,)), dma((2, CHUNKS)), dma(()), dma((n_rows,)), dma((2,)), dma((2,)),
        ],
        compiler_params=pltpu.CompilerParams(
            collective_id=2 * tick + 1, has_side_effects=True, vmem_limit_bytes=VMEM),
        cost_estimate=pl.CostEstimate(flops=10**10, bytes_accessed=10**7, transcendentals=0),
    )(v, own, sib, weights)


def pick_kernel(plan, w_in, w_out, first, second, sem):
    section = lax.axis_index("section")
    core = lax.rem(lax.axis_index("lon"), 2)
    shard, ff = w_in.shape[2], w_in.shape[3] // 2
    columns = pl.ds(pl.multiple_of(core * ff, ff), ff)
    copies = [
        pltpu.make_async_copy(ref.at[0, plan[tick, section], :, columns], out.at[pl.ds(k * shard, shard)], sem.at[tick, k])
        for tick, out in enumerate((first, second))
        for k, ref in enumerate((w_in, w_out))
    ]
    for copy in copies:
        copy.start()
    for copy in copies:
        copy.wait()


def own_weights(plan, w_in, w_out):
    anys = pl.BlockSpec(memory_space=pltpu.HBM)
    out = jax.ShapeDtypeStruct((2 * w_in.shape[2], w_in.shape[3] // 2), BF16)
    return pl.pallas_call(
        pick_kernel,
        out_shape=(out, out),
        in_specs=[pl.BlockSpec(memory_space=pltpu.SMEM), anys, anys],
        out_specs=(pl.BlockSpec(memory_space=pltpu.VMEM),) * 2,
        scratch_shapes=[pltpu.SemaphoreType.DMA((2, 2))],
        compiler_params=pltpu.CompilerParams(vmem_limit_bytes=VMEM),
    )(plan, w_in, w_out)


def local(state, fresh, cutoff, plan, lmax, mmax, cutoff_table, norm_gains, filters, w_in, w_out):
    n_section = lax.axis_size("section")
    n_lat = lax.axis_size("lat")
    n_lon = lax.axis_size("lon")
    n_rows, n_cols, width = fresh.shape
    n_degrees = filters.shape[3]
    tables = [jnp.asarray(t) for t in spectral_tables(n_lat, n_lon, n_rows, n_cols, n_degrees)]
    weights = [lax.all_gather(mine, "lat", axis=0) for mine in own_weights(plan, w_in, w_out)]
    other_gains = passed_along(norm_gains, "section", -1)

    def spectral(tick, tokens, *more):
        return spectral_part(
            tick, n_section, plan, cutoff, lmax, mmax, tokens, cutoff_table, norm_gains, filters, tables, more)

    *parts, entering = spectral(0, state[0], fresh)
    first_out = mlp_part(0, *parts, weights[0])
    parts = spectral(1, fresh, first_out, other_gains, entering)
    second_out = mlp_part(1, *parts, weights[1])
    return (first_out[None], second_out[None])


def solution(mesh):
    return jax.shard_map(
        local,
        mesh=mesh,
        in_specs=(
            P("section", "lat", "lon", None),
            P("lat", "lon", None),
            P(),
            P(),
            P(),
            P(),
            P(),
            P("section", None, None, None),
            P("section", None, None, None, "lon"),
            P("section", None, "lat", None),
            P("section", None, "lat", None),
        ),
        out_specs=(P("section", "lat", "lon", None), P("section", "lat", "lon", None)),
        check_vma=False,
    )
```

```python
import functools
import math

import jax
import jax.numpy as jnp
import numpy as np
from jax import lax
from jax.experimental import pallas as pl
from jax.experimental.pallas import tpu as pltpu
from jax.sharding import PartitionSpec as P

MM = 96
MESH = pl.DeviceIdType.MESH
BF16 = jnp.bfloat16
F32 = jnp.float32
VMEM = 60 * 1024 * 1024
LON_PAD = 96
MODE_PAD = 16
GROUPS = ((0, 4), (4, 3))
ROWS = ((0, 2), (2, 2), (4, 3))


def passed_along(value, axis, steps):
    count = lax.axis_size(axis)
    leading, last = (max(0, -steps), min(count, count - steps))
    return lax.ppermute(value, axis, [(source, source + steps) for source in range(leading, last)])


def legendre_table(n_orders, n_rows, n_degrees):
    theta = math.pi * (np.arange(n_rows) + 0.5) / n_rows
    cosine, sine = np.cos(theta), np.sin(theta)
    table = np.zeros((n_degrees, n_orders, n_rows))
    for m in range(n_orders):
        log_start = (
            0.5 * math.log((2.0 * m + 1.0) / (4.0 * math.pi))
            + math.lgamma(m + 0.5) - math.lgamma(0.5) - math.lgamma(m + 1.0)
        )
        table[m, m] = np.exp(log_start + m * np.log(sine))
        for l in range(m + 1, n_degrees):
            coef_a = math.sqrt((4.0 * l * l - 1.0) / (l * l - m * m))
            coef_b = math.sqrt(max((l - 1.0) ** 2 - m * m, 0.0) / max(4.0 * (l - 1.0) ** 2 - 1.0, 1.0))
            before = table[l - 2, m] if l - 2 >= m else 0.0
            table[l, m] = coef_a * (cosine * table[l - 1, m] - coef_b * before)
    quad = 2.0 * math.pi * (math.pi / n_rows) * sine
    return table, table * quad


def spectral_tables(n_lat, n_lon, n_rows, n_cols, n_degrees):
    m_local = MM // n_lat
    all_cols = n_cols * n_lon
    phase = 2.0 * math.pi * ((np.arange(all_cols)[:, None] * np.arange(MM)[None, :]) % all_cols) / all_cols
    weight = np.where(np.arange(MM) == 0, 1.0, 2.0)
    forward = np.zeros((n_lat, MODE_PAD, n_lon, LON_PAD))
    inverse = np.zeros((n_lon, LON_PAD, n_lat, MODE_PAD))
    parts = ((np.cos(phase) / all_cols, weight * np.cos(phase)), (-np.sin(phase) / all_cols, -weight * np.sin(phase)))
    for r, (fwd, inv) in enumerate(parts):
        fwd = fwd.reshape(n_lon, n_cols, n_lat, m_local)
        inv = inv.reshape(n_lon, n_cols, n_lat, m_local)
        forward[:, r * m_local : (r + 1) * m_local, :, :n_cols] = fwd.transpose(2, 3, 0, 1)
        inverse[:, :n_cols, :, r * m_local : (r + 1) * m_local] = inv
    forward = forward.reshape(n_lat * MODE_PAD, n_lon * LON_PAD)
    inverse = inverse.reshape(n_lon * LON_PAD, n_lat * MODE_PAD)
    plain, weighted = legendre_table(MM, n_rows * n_lat, n_degrees)
    split = (n_degrees, n_lat, m_local, n_lat, n_rows)
    weighted = weighted.reshape(split).transpose(1, 2, 0, 3, 4).reshape(n_lat, m_local, n_degrees, n_lat * n_rows)
    padded = np.zeros((n_lat, m_local, n_lat, 8, n_degrees))
    padded[:, :, :, :n_rows] = plain.reshape(split).transpose(1, 2, 3, 4, 0)
    padded = padded.reshape(n_lat, m_local, n_lat * 8, n_degrees)
    return tuple(t.astype(BF16) for t in (forward, inverse, weighted, padded))


def normed_parts(values):
    scale = 1.0 / values.shape[-1]
    mean = jnp.sum(values, axis=-1, keepdims=True) * scale
    center = values - mean
    spread = jnp.sum(center * center, axis=-1, keepdims=True) * scale
    return center, mean, lax.rsqrt(spread + 1e-05)


def layer_norm(values, gain):
    center, _, scale = normed_parts(values)
    return center * scale * gain


def lon_peer(me, d):
    return lax.rem(me // 2 + d // 2, 2) * 2 + lax.rem(lax.rem(me, 2) + d % 2, 2)


def spec_kernel(
    tick, n_section, plan, cutoff, lmax, mmax, *refs,
):
    if tick == 0:
        tok_hbm, prior_hbm, *refs = refs
    else:
        tok_hbm, prior_hbm, other_gains, x_next, *refs = refs
    cut_table, gains, filters, fwd, inv, leg_hbm, legt_hbm, v_out, own_out, sib_out, *refs = refs
    if tick == 0:
        x_next, *refs = refs
    (
        tok, prior, norm, ahead, x_all, spec, y_all, y_f32, f_f32, back, z_all, o_all, r_all, vbuf, nbuf, leg, legt,
        a_send, a_recv, e_send, f_recv, t_send, t_recv, b_send, b_recv, c_send, c_recv, d_send, d_recv, n_send, n_recv, loc, row_in, next_sem,
        stat, stat_in, stat_sem,
    ) = refs
    section, lat, lon = (lax.axis_index(a) for a in ("section", "lat", "lon"))
    n_lat = spec.shape[1]
    n_rows, n_cols, width = tok.shape
    n_degrees, part = filters.shape[3], filters.shape[4]
    m_local = leg.shape[0]
    half = part // 2
    sibling = lon_peer(lon, 1)
    handing = tick > 0
    first_section = section == 0

    barrier = pltpu.get_barrier_semaphore()
    greeted = 3 + n_lat - 1
    for d in (1, 2, 3):
        pl.semaphore_signal(barrier, inc=1, device_id={"lon": lon_peer(lon, d)}, device_id_type=MESH)
    if handing:
        greeted += 4
        for q in range(4):
            pl.semaphore_signal(barrier, inc=1, device_id={"section": 1 - section, "lon": q}, device_id_type=MESH)

    def greet(d, carry):
        pl.semaphore_signal(barrier, inc=1, device_id={"lat": lax.rem(lat + d, n_lat)}, device_id_type=MESH)
        return carry

    lax.fori_loop(1, n_lat, greet, 0)

    def get_tok(j):
        return pltpu.make_async_copy(tok_hbm.at[j], tok.at[j], row_in.at[0, j])

    def get_prior(j):
        return pltpu.make_async_copy(prior_hbm.at[j], prior.at[j], row_in.at[1, j])

    def get_next(h):
        return pltpu.make_async_copy(x_next.at[h], x_all.at[h], next_sem.at[h])

    def put_next(h):
        return pltpu.make_async_copy(ahead.at[h, lon], x_next.at[h, lon], next_sem.at[h])

    def over_rows(step):
        def body(j, carry):
            step(j)
            return carry

        lax.fori_loop(0, n_rows, body, 0)

    if handing:

        @pl.when(first_section)
        def _():
            over_rows(lambda j: get_prior(j).start())
            for h in (0, 1):
                get_next(h).start()
            over_rows(lambda j: get_tok(j).start())
    else:
        over_rows(lambda j: get_tok(j).start())

        @pl.when(first_section)
        def _():
            over_rows(lambda j: get_prior(j).start())
    get_leg = pltpu.make_async_copy(leg_hbm.at[lat], leg, loc.at[0])
    get_legt = pltpu.make_async_copy(legt_hbm.at[lat], legt, loc.at[1])
    get_leg.start()
    get_legt.start()

    block = plan[tick, section]
    cut = cutoff[tick - section + n_section - 1]
    l_max, m_max = lmax[section], mmax[section]
    embed = cut_table[pl.ds(cut, 1), :]
    gain_one = gains[0, block, 0:1, :]
    gain_two = gains[0, block, 1:2, :]
    pad = jnp.zeros((2, 4, n_rows, 16, half), BF16)
    ahead[:, :, :, LON_PAD - 16 :, :] = pad
    if not handing:
        norm[:, :, :, LON_PAD - 16 :, :] = pad
    f_f32[...] = jnp.zeros_like(f_f32)
    nbuf[:, LON_PAD - 16 :, :] = jnp.zeros((n_rows, 16, width), BF16)
    pl.semaphore_wait(barrier, greeted)

    def copy_a(h, j, d, sending):
        peer = lon_peer(lon, d)
        slot = lon if sending else peer
        return pltpu.make_async_remote_copy(
            src_ref=norm.at[h, peer, j] if sending else x_all.at[h, slot, j], dst_ref=x_all.at[h, slot, j], send_sem=a_send.at[h, d, j],
            recv_sem=a_recv.at[h, d, j], device_id={"lon": peer}, device_id_type=MESH)

    def copy_e(h, j, d):
        peer = lon_peer(lon, d)
        return pltpu.make_async_remote_copy(
            src_ref=ahead.at[h, peer, j], dst_ref=x_all.at[h, lon, j], send_sem=e_send.at[h, d, j],
            recv_sem=a_recv.at[h, d, j], device_id={"section": 1 - section, "lon": peer}, device_id_type=MESH)

    def copy_f(h, j, d, sending):
        peer = lon_peer(lon, d)
        slot = lon if sending else peer
        return pltpu.make_async_remote_copy(
            src_ref=ahead.at[h, peer, j], dst_ref=x_next.at[h, slot, j], send_sem=e_send.at[h, d, j],
            recv_sem=f_recv.at[h, d, j], device_id={"lon": peer}, device_id_type=MESH)

    def copy_t(d):
        quarter = pl.ds(pl.multiple_of(lon_peer(lon, d) * part, part), part)
        return pltpu.make_async_remote_copy(
            src_ref=prior.at[:, :, quarter], dst_ref=tok.at[:, :, quarter], send_sem=t_send.at[d], recv_sem=t_recv.at[d],
            device_id={"section": 1 - section}, device_id_type=MESH)

    def copy_stat():
        return pltpu.make_async_remote_copy(
            src_ref=stat, dst_ref=stat_in, send_sem=stat_sem.at[0], recv_sem=stat_sem.at[1],
            device_id={"section": 1 - section}, device_id_type=MESH)

    def split_into(dst, j, out):
        for q in range(4):
            for h in (0, 1):
                at = q * part + h * half
                dst[h, q, j, 0:n_cols, :] = out[:, at : at + half]

    def first_norm(j):
        get_tok(j).wait()
        split_into(norm, j, layer_norm(tok[j].astype(F32) + embed, gain_one).astype(BF16))
        for d in (2, 3, 1):
            copy_a(0, j, d, True).start()
        for h in (0, 1):
            x_all[h, lon, j] = norm[h, lon, j]

    def first_norm_rest(j):
        for d in (2, 3, 1):
            copy_a(1, j, d, True).start()

    if handing:

        @pl.when(first_section)
        def _():
            next_block = plan[tick, 1]
            next_embed = cut_table[pl.ds(cutoff[tick - 1 + n_section - 1], 1), :]
            next_gain = other_gains[0, next_block, 0:1, :]

            stat[...] = jnp.zeros_like(stat)
            lane = lax.broadcasted_iota(jnp.int32, (n_cols, stat.shape[1]), 1)

            def norm_ahead(j):
                get_prior(j).wait()
                raw = prior[j].astype(F32)
                center, mean, scale = normed_parts(raw + next_embed)
                out = center * scale * next_gain
                for q in range(4):
                    at = slice(q * part, (q + 1) * part)
                    mixed = jnp.where(lon == q, raw[:, at], out[:, at]).astype(BF16)
                    for h in (0, 1):
                        ahead[h, q, j, 0:n_cols, :] = mixed[:, h * half : (h + 1) * half]
                for d in range(4):
                    copy_e(0, j, d).start()
                old = stat[0:n_cols, :]
                stat[0:n_cols, :] = jnp.where(lane == 2 * j, mean, jnp.where(lane == 2 * j + 1, scale, old))

            def norm_ahead_rest(j):
                for d in range(4):
                    copy_e(1, j, d).start()

            over_rows(norm_ahead)
            copy_stat().start()
            over_rows(norm_ahead_rest)
            for d in (1, 2, 3):
                copy_t(d).start()
    else:
        over_rows(first_norm)
        over_rows(first_norm_rest)

        @pl.when(first_section)
        def _():
            next_block = plan[tick + 1, 0]
            next_embed = cut_table[pl.ds(cutoff[tick + 1 + n_section - 1], 1), :]
            next_gain = gains[0, next_block, 0:1, :]

            def norm_next(j):
                get_prior(j).wait()
                split_into(ahead, j, layer_norm(prior[j].astype(F32) + next_embed, next_gain).astype(BF16))
                for h in (0, 1):
                    for d in (2, 3, 1):
                        copy_f(h, j, d, True).start()

            over_rows(norm_next)
            for h in (0, 1):
                put_next(h).start()

    def moved(src, dst, send, recv, sending, h, d):
        peer = lax.rem(lat + d, n_lat)
        origin = lax.rem(lat - d + n_lat, n_lat)
        where = lat if sending else origin
        return pltpu.make_async_remote_copy(
            src_ref=src.at[h, peer], dst_ref=dst.at[h, where],
            send_sem=send.at[h, d], recv_sem=recv.at[h, d], device_id={"lat": peer}, device_id_type=MESH)

    def over_lat(step):
        def body(d, carry):
            step(d)
            return carry

        lax.fori_loop(1, n_lat, body, 0)

    def take_a(h, j):
        for d in (1, 2, 3):
            copy_a(h, j, d, False).wait_recv()

    def of_lon(row, h):
        out = row[:, h * half : (h + 1) * half]
        for q in (1, 2, 3):
            out = jnp.where(lon == q, row[:, q * part + h * half : q * part + (h + 1) * half], out)
        return out

    def arrived(h, j):
        if not handing:
            return x_all[h, :, j].reshape(4 * LON_PAD, half)
        shift, gain = of_lon(embed, h), of_lon(gain_one, h)
        own = x_all[h, lon, j].astype(F32)
        own = (own + shift - stat_in[:, 2 * j : 2 * j + 1]) * stat_in[:, 2 * j + 1 : 2 * j + 2] * gain
        rows_of = []
        for q in range(4):
            is_raw = jnp.logical_and(section > 0, lon == q)
            rows_of.append(jnp.where(is_raw, own, x_all[h, q, j].astype(F32)).astype(BF16))
        return jnp.concatenate(rows_of, axis=0)

    def zonal(h, first, count):
        if handing:

            @pl.when(jnp.logical_not(first_section))
            def _():
                for j in range(first, first + count):
                    copy_e(h, j, 0).wait_recv()
                    take_a(h, j)
        else:
            for j in range(first, first + count):
                take_a(h, j)

        wide = jnp.concatenate([arrived(h, j) for j in range(first, first + count)], axis=1)
        out = jnp.dot(fwd[...], wide, preferred_element_type=F32).astype(BF16)
        for i in range(count):
            spec[h, :, first + i] = out[:, i * half : (i + 1) * half].reshape(n_lat, MODE_PAD, half)

    for h in (0, 1):
        if handing:

            @pl.when(first_section)
            def _(h=h):
                get_next(h).wait()

            if h == 0:

                @pl.when(jnp.logical_not(first_section))
                def _():
                    copy_stat().wait_recv()

        for first, count in ROWS:
            zonal(h, first, count)
        over_lat(lambda d, h=h: moved(spec, y_all, b_send, b_recv, True, h, d).start())

    rows = n_rows * MODE_PAD
    n_lines = n_lat * n_rows
    degree = lax.broadcasted_iota(jnp.int32, (n_degrees, half), 0)
    get_leg.wait()
    get_legt.wait()

    for h in (0, 1):

        def widen(src, value, h=h):
            at = pl.multiple_of(src * rows, 16)
            y_f32[h, pl.ds(at, rows), :] = value.reshape(rows, half).astype(F32)

        widen(lat, spec[h, lat])

        def take_b(d, h=h):
            moved(spec, y_all, b_send, b_recv, False, h, d).wait_recv()
            origin = lax.rem(lat - d + n_lat, n_lat)
            widen(origin, y_all[h, origin])

        over_lat(take_b)
        fil_re = filters[0, block, 0, :, h * half : (h + 1) * half]
        fil_im = filters[0, block, 1, :, h * half : (h + 1) * half]
        for m in range(m_local):
            pieces = [y_f32[h, pl.ds(r * m_local + m, n_lines, stride=MODE_PAD), :] for r in (0, 1)]
            column = jnp.concatenate(pieces, axis=1).astype(BF16)
            coeff = jnp.dot(leg[m], column, preferred_element_type=F32)
            co_re, co_im = coeff[:, :half], coeff[:, half:]
            order = lat * m_local + m
            keep = (degree < l_max) & (jnp.full((n_degrees, half), order, jnp.int32) < m_max)
            out_re = jnp.where(keep, co_re * fil_re - co_im * fil_im, 0.0)
            out_im = jnp.where(keep, co_re * fil_im + co_im * fil_re, 0.0)
            out = jnp.concatenate([out_re, out_im], axis=1).astype(BF16)
            lines = jnp.dot(legt[m], out, preferred_element_type=F32)
            for r in (0, 1):
                f_f32[h, pl.ds(r * m_local + m, n_lat * 8, stride=MODE_PAD), :] = lines[:, r * half : (r + 1) * half]

        def narrow(peer, h=h):
            at = pl.multiple_of(peer * (8 * MODE_PAD), 16)
            return f_f32[h, pl.ds(at, rows), :].astype(BF16).reshape(n_rows, MODE_PAD, half)

        def send_c(d, h=h):
            peer = lax.rem(lat + d, n_lat)
            back[h, peer] = narrow(peer)
            moved(back, z_all, c_send, c_recv, True, h, d).start()

        over_lat(send_c)
        z_all[h, lat] = narrow(lat)

    def copy_d(h, j, d, sending):
        peer = lon_peer(lon, d)
        slot = lon if sending else peer
        return pltpu.make_async_remote_copy(
            src_ref=o_all.at[h, peer, j], dst_ref=r_all.at[h, slot, j], send_sem=d_send.at[h, d, j],
            recv_sem=d_recv.at[h, d, j], device_id={"lon": peer}, device_id_type=MESH)

    for h in (0, 1):
        over_lat(lambda d, h=h: moved(back, z_all, c_send, c_recv, False, h, d).wait_recv())
        for first, count in ROWS:
            modes = jnp.concatenate(
                [z_all[h, :, j].reshape(n_lat * MODE_PAD, half) for j in range(first, first + count)], axis=1)
            out = jnp.dot(inv[...], modes, preferred_element_type=F32).astype(BF16)
            for i in range(count):
                j = first + i
                o_all[h, :, j] = out[:, i * half : (i + 1) * half].reshape(4, LON_PAD, half)
                for d in (2, 3, 1):
                    copy_d(h, j, d, True).start()
                r_all[h, lon, j] = o_all[h, lon, j]

    def put_v(j):
        return pltpu.make_async_copy(vbuf.at[j], v_out.at[j], loc.at[2 + j])

    def put_own(j):
        return pltpu.make_async_copy(nbuf.at[j], own_out.at[j], loc.at[2 + n_rows + j])

    def put_sib(j):
        return pltpu.make_async_remote_copy(
            src_ref=nbuf.at[j], dst_ref=sib_out.at[j], send_sem=n_send.at[j], recv_sem=n_recv.at[j],
            device_id={"lon": sibling}, device_id_type=MESH)

    if handing:

        @pl.when(jnp.logical_not(first_section))
        def _():
            for d in (1, 2, 3):
                copy_t(d).wait_recv()

            def assemble(j):
                for h in (0, 1):
                    mine = pl.ds(pl.multiple_of(lon * part + h * half, half), half)
                    tok[j, :, mine] = x_all[h, lon, j, 0:n_cols, :]

            over_rows(assemble)

        @pl.when(first_section)
        def _():
            over_rows(lambda j: get_tok(j).wait())

    def second_norm(j):
        for h in (0, 1):
            for d in (1, 2, 3):
                copy_d(h, j, d, False).wait_recv()
        spectral = jnp.concatenate(
            [r_all[h, q, j, 0:n_cols, :] for q in range(4) for h in (0, 1)], axis=1).astype(F32)
        mixed = tok[j].astype(F32) + embed + spectral
        vbuf[j] = mixed
        nbuf[j, 0:n_cols, :] = layer_norm(mixed, gain_two).astype(BF16)
        put_sib(j).start()
        put_v(j).start()
        put_own(j).start()

    over_rows(second_norm)

    def finish_a(j):
        for h in (0, 1):
            for d in (1, 2, 3):
                copy_a(h, j, d, True).wait_send()

    def finish_rows(j):
        for h in (0, 1):
            for d in (1, 2, 3):
                copy_d(h, j, d, True).wait_send()
        put_v(j).wait()
        put_own(j).wait()
        put_sib(j).wait()

    def finish_lat(d):
        for h in (0, 1):
            moved(spec, y_all, b_send, b_recv, True, h, d).wait_send()
            moved(back, z_all, c_send, c_recv, True, h, d).wait_send()

    if handing:

        def finish_handing(j):
            for h in (0, 1):
                for d in range(4):
                    copy_e(h, j, d).wait_send()

        @pl.when(first_section)
        def _():
            over_rows(finish_handing)
            copy_stat().wait_send()
            for d in (1, 2, 3):
                copy_t(d).wait_send()
    else:

        def finish_next(j):
            for h in (0, 1):
                for d in (1, 2, 3):
                    copy_f(h, j, d, True).wait_send()
                    copy_f(h, j, d, False).wait_recv()

        @pl.when(first_section)
        def _():
            over_rows(finish_next)
            for h in (0, 1):
                put_next(h).wait()

        over_rows(finish_a)
    over_lat(finish_lat)
    over_rows(finish_rows)


def spectral_part(tick, n_section, plan, cutoff, lmax, mmax, tokens, cut_table, gains, filters, tables, prior=()):
    n_rows, n_cols, width = tokens.shape
    fwd, inv, leg, legt = tables
    n_lat, m_local, n_degrees, n_lines = leg.shape
    part = filters.shape[4]
    half = part // 2
    smem = pl.BlockSpec(memory_space=pltpu.SMEM)
    vmem = pl.BlockSpec(memory_space=pltpu.VMEM)
    anys = pl.BlockSpec(memory_space=pltpu.HBM)
    dma = pltpu.SemaphoreType.DMA
    lonwise = pltpu.VMEM((2, 4, n_rows, LON_PAD, half), BF16)
    latwise = pltpu.VMEM((2, n_lat, n_rows, MODE_PAD, half), BF16)
    small = pltpu.VMEM((16, 128), BF16)
    tokens_buf = pltpu.VMEM((n_rows, n_cols, width), BF16)
    return pl.pallas_call(
        functools.partial(spec_kernel, tick, n_section),
        out_shape=(
            jax.ShapeDtypeStruct((n_rows, n_cols, width), F32),
            jax.ShapeDtypeStruct((n_rows, LON_PAD, width), BF16),
            jax.ShapeDtypeStruct((n_rows, LON_PAD, width), BF16),
        ) + (() if tick else (jax.ShapeDtypeStruct(lonwise.shape, BF16),)),
        in_specs=[smem] * 4 + [anys] * 2 + ([vmem, anys] if tick else []) + [vmem] * 5 + [anys] * 2,
        out_specs=(anys,) * (3 if tick else 4),
        scratch_shapes=[
            tokens_buf, tokens_buf, small if tick else lonwise, lonwise, lonwise, latwise, latwise,
            pltpu.VMEM((2, n_lines * MODE_PAD, half), F32),
            pltpu.VMEM((2, n_lat * 8 * MODE_PAD, half), F32),
            latwise, latwise, lonwise, lonwise,
            pltpu.VMEM((n_rows, n_cols, width), F32),
            pltpu.VMEM((n_rows, LON_PAD, width), BF16),
            pltpu.VMEM(leg.shape[1:], BF16),
            pltpu.VMEM(legt.shape[1:], BF16),
            dma((2, 4, n_rows)), dma((2, 4, n_rows)), dma((2, 4, n_rows)), dma((2, 4, n_rows)),
            dma((4,)), dma((4,)),
            dma((2, n_lat)), dma((2, n_lat)),
            dma((2, n_lat)), dma((2, n_lat)),
            dma((2, 4, n_rows)), dma((2, 4, n_rows)),
            dma((n_rows,)), dma((n_rows,)),
            dma((2 + 2 * n_rows,)), dma((2, n_rows)), dma((2,)),
            pltpu.VMEM((LON_PAD, 128), F32),
            pltpu.VMEM((LON_PAD, 128), F32),
            dma((2,)),
        ],
        compiler_params=pltpu.CompilerParams(
            collective_id=2 * tick, has_side_effects=True, vmem_limit_bytes=VMEM),
        cost_estimate=pl.CostEstimate(flops=5 * 10**10, bytes_accessed=10**7, transcendentals=0),
    )(plan, cutoff, lmax, mmax, tokens, *prior, cut_table, gains, filters, fwd, inv, leg, legt)


CHUNKS = 2
LATER = 2


def mlp_kernel(
    v_hbm, own_hbm, sib_hbm, w_hbm, out_hbm,
    x_all, wi, wo, acc, given, taken, vbuf, obuf, x_sem, w_sem, v_sem, o_sem, p_send, p_recv,
):
    lon = lax.axis_index("lon")
    sibling = lon_peer(lon, 1)
    n_rows, n_cols, width = v_hbm.shape
    ff = wi.shape[2]
    part = ff // CHUNKS
    shard = w_hbm.shape[1] // 2

    barrier = pltpu.get_barrier_semaphore()
    pl.semaphore_signal(barrier, inc=1, device_id={"lon": sibling}, device_id_type=MESH)

    get_x = [
        pltpu.make_async_copy(ref.at[pl.ds(first, count)], x_all.at[pl.ds(n_rows * k + first, count)], x_sem.at[2 * k + g])
        for k, ref in enumerate((sib_hbm, own_hbm))
        for g, (first, count) in enumerate(GROUPS)
    ]

    def get_wi(c):
        return pltpu.make_async_copy(w_hbm.at[:, pl.ds(0, shard), pl.ds(c * part, part)], wi.at[:, :, pl.ds(c * part, part)], w_sem.at[0, c])

    def get_wo(c):
        return pltpu.make_async_copy(w_hbm.at[:, pl.ds(shard, shard), pl.ds(c * part, part)], wo.at[:, :, pl.ds(c * part, part)], w_sem.at[1, c])

    get_v = pltpu.make_async_copy(v_hbm, vbuf, v_sem)
    get_x[0].start()
    for c in range(CHUNKS):
        get_wi(c).start()
        get_wo(c).start()
        if c == 0:
            get_x[1].start()
    get_x[2].start()
    get_x[3].start()
    get_v.start()
    pl.semaphore_wait(barrier, 1)

    def send(g):
        first, count = GROUPS[g]
        return pltpu.make_async_remote_copy(
            src_ref=given.at[pl.ds(first, count)], dst_ref=taken.at[pl.ds(first, count)],
            send_sem=p_send.at[g], recv_sem=p_recv.at[g], device_id={"lon": sibling}, device_id_type=MESH)

    def put(j):
        return pltpu.make_async_copy(obuf.at[j], out_hbm.at[j], o_sem.at[j])

    for tile in range(4):
        k, g = tile // 2, tile % 2
        first, count = GROUPS[g]
        size = count * LON_PAD
        get_x[tile].wait()

        x = x_all[pl.ds(n_rows * k + first, count)].reshape(size, width)
        pieces = CHUNKS if tile == 0 else LATER
        wide = ff // pieces
        for c in range(pieces):
            if tile == 0:
                get_wi(c).wait()
            at = c * wide
            before = jnp.dot(x, wi[:, :, at : at + wide].reshape(width, wide), preferred_element_type=F32)
            h = jax.nn.gelu(before).astype(BF16)
            if tile == 0:
                get_wo(c).wait()
            out = lax.dot_general(
                h, wo[:, :, at : at + wide].reshape(width, wide), (((1,), (1,)), ((), ())), preferred_element_type=F32)
            acc[0:size, :] = out if c == 0 else acc[0:size, :] + out
        total = acc[0:size, :].reshape(count, LON_PAD, width)
        if k == 0:
            given[pl.ds(first, count)] = total.astype(BF16)
            send(g).start()
        else:
            if g == 0:
                get_v.wait()
            send(g).wait_recv()
            for i in range(count):
                j = first + i
                other = taken[j, 0:n_cols, :].astype(F32)
                obuf[j] = (vbuf[j] + (total[i, 0:n_cols, :] + other)).astype(BF16)
                put(j).start()
    for j in range(n_rows):
        put(j).wait()
    for g in range(2):
        send(g).wait_send()


def mlp_part(tick, v, own, sib, weights):
    n_rows, n_cols, width = v.shape
    n_lat, shard, ff = weights.shape
    shard = shard // 2
    anys = pl.BlockSpec(memory_space=pltpu.HBM)
    dma = pltpu.SemaphoreType.DMA
    most = max(count for _, count in GROUPS)
    return pl.pallas_call(
        mlp_kernel,
        out_shape=jax.ShapeDtypeStruct((n_rows, n_cols, width), BF16),
        in_specs=[anys] * 4,
        out_specs=anys,
        scratch_shapes=[
            pltpu.VMEM((2 * n_rows, LON_PAD, width), BF16),
            pltpu.VMEM((n_lat, shard, ff), BF16),
            pltpu.VMEM((n_lat, shard, ff), BF16),
            pltpu.VMEM((most * LON_PAD, width), F32),
            pltpu.VMEM((n_rows, LON_PAD, width), BF16),
            pltpu.VMEM((n_rows, LON_PAD, width), BF16),
            pltpu.VMEM((n_rows, n_cols, width), F32),
            pltpu.VMEM((n_rows, n_cols, width), BF16),
            dma((4,)), dma((2, CHUNKS)), dma(()), dma((n_rows,)), dma((2,)), dma((2,)),
        ],
        compiler_params=pltpu.CompilerParams(
            collective_id=2 * tick + 1, has_side_effects=True, vmem_limit_bytes=VMEM),
        cost_estimate=pl.CostEstimate(flops=10**10, bytes_accessed=10**7, transcendentals=0),
    )(v, own, sib, weights)


def pick_kernel(tick, plan, w_in, w_out, out, sem):
    section = lax.axis_index("section")
    core = lax.rem(lax.axis_index("lon"), 2)
    shard, ff = w_in.shape[2], w_in.shape[3] // 2
    columns = pl.ds(pl.multiple_of(core * ff, ff), ff)
    copies = [
        pltpu.make_async_copy(ref.at[0, plan[tick, section], :, columns], out.at[pl.ds(k * shard, shard)], sem.at[k])
        for k, ref in enumerate((w_in, w_out))
    ]
    for copy in copies:
        copy.start()
    for copy in copies:
        copy.wait()


def own_weights(tick, plan, w_in, w_out):
    anys = pl.BlockSpec(memory_space=pltpu.HBM)
    out = jax.ShapeDtypeStruct((2 * w_in.shape[2], w_in.shape[3] // 2), BF16)
    return pl.pallas_call(
        functools.partial(pick_kernel, tick),
        out_shape=out,
        in_specs=[pl.BlockSpec(memory_space=pltpu.SMEM), anys, anys],
        out_specs=pl.BlockSpec(memory_space=pltpu.VMEM),
        scratch_shapes=[pltpu.SemaphoreType.DMA((2,))],
        compiler_params=pltpu.CompilerParams(vmem_limit_bytes=VMEM),
    )(plan, w_in, w_out)


def local(state, fresh, cutoff, plan, lmax, mmax, cutoff_table, norm_gains, filters, w_in, w_out):
    n_section = lax.axis_size("section")
    n_lat = lax.axis_size("lat")
    n_lon = lax.axis_size("lon")
    n_rows, n_cols, width = fresh.shape
    n_degrees = filters.shape[3]
    tables = [jnp.asarray(t) for t in spectral_tables(n_lat, n_lon, n_rows, n_cols, n_degrees)]
    weights = [lax.all_gather(own_weights(tick, plan, w_in, w_out), "lat", axis=0) for tick in (0, 1)]
    other_gains = passed_along(norm_gains, "section", -1)

    def spectral(tick, tokens, *more):
        return spectral_part(
            tick, n_section, plan, cutoff, lmax, mmax, tokens, cutoff_table, norm_gains, filters, tables, more)

    *parts, entering = spectral(0, state[0], fresh)
    first_out = mlp_part(0, *parts, weights[0])
    parts = spectral(1, fresh, first_out, other_gains, entering)
    second_out = mlp_part(1, *parts, weights[1])
    return (first_out[None], second_out[None])


def solution(mesh):
    return jax.shard_map(
        local,
        mesh=mesh,
        in_specs=(
            P("section", "lat", "lon", None),
            P("lat", "lon", None),
            P(),
            P(),
            P(),
            P(),
            P(),
            P("section", None, None, None),
            P("section", None, None, None, "lon"),
            P("section", None, "lat", None),
            P("section", None, "lat", None),
        ),
        out_specs=(P("section", "lat", "lon", None), P("section", "lat", "lon", None)),
        check_vma=False,
    )
```

```python
import functools
import math

import jax
import jax.numpy as jnp
import numpy as np
from jax import lax
from jax.experimental import pallas as pl
from jax.experimental.pallas import tpu as pltpu
from jax.sharding import PartitionSpec as P

MM = 96
MESH = pl.DeviceIdType.MESH
BF16 = jnp.bfloat16
F32 = jnp.float32
VMEM = 60 * 1024 * 1024
LON_PAD = 96
MODE_PAD = 16
GROUPS = ((0, 4), (4, 3))
ROWS = ((0, 2), (2, 2), (4, 3))


def passed_along(value, axis, steps):
    count = lax.axis_size(axis)
    leading, last = (max(0, -steps), min(count, count - steps))
    return lax.ppermute(value, axis, [(source, source + steps) for source in range(leading, last)])


def legendre_table(n_orders, n_rows, n_degrees):
    theta = math.pi * (np.arange(n_rows) + 0.5) / n_rows
    cosine, sine = np.cos(theta), np.sin(theta)
    table = np.zeros((n_degrees, n_orders, n_rows))
    for m in range(n_orders):
        log_start = (
            0.5 * math.log((2.0 * m + 1.0) / (4.0 * math.pi))
            + math.lgamma(m + 0.5) - math.lgamma(0.5) - math.lgamma(m + 1.0)
        )
        table[m, m] = np.exp(log_start + m * np.log(sine))
        for l in range(m + 1, n_degrees):
            coef_a = math.sqrt((4.0 * l * l - 1.0) / (l * l - m * m))
            coef_b = math.sqrt(max((l - 1.0) ** 2 - m * m, 0.0) / max(4.0 * (l - 1.0) ** 2 - 1.0, 1.0))
            before = table[l - 2, m] if l - 2 >= m else 0.0
            table[l, m] = coef_a * (cosine * table[l - 1, m] - coef_b * before)
    quad = 2.0 * math.pi * (math.pi / n_rows) * sine
    return table, table * quad


def spectral_tables(n_lat, n_lon, n_rows, n_cols, n_degrees):
    m_local = MM // n_lat
    all_cols = n_cols * n_lon
    phase = 2.0 * math.pi * ((np.arange(all_cols)[:, None] * np.arange(MM)[None, :]) % all_cols) / all_cols
    weight = np.where(np.arange(MM) == 0, 1.0, 2.0)
    forward = np.zeros((n_lat, MODE_PAD, n_lon, LON_PAD))
    inverse = np.zeros((n_lon, LON_PAD, n_lat, MODE_PAD))
    parts = ((np.cos(phase) / all_cols, weight * np.cos(phase)), (-np.sin(phase) / all_cols, -weight * np.sin(phase)))
    for r, (fwd, inv) in enumerate(parts):
        fwd = fwd.reshape(n_lon, n_cols, n_lat, m_local)
        inv = inv.reshape(n_lon, n_cols, n_lat, m_local)
        forward[:, r * m_local : (r + 1) * m_local, :, :n_cols] = fwd.transpose(2, 3, 0, 1)
        inverse[:, :n_cols, :, r * m_local : (r + 1) * m_local] = inv
    forward = forward.reshape(n_lat * MODE_PAD, n_lon * LON_PAD)
    inverse = inverse.reshape(n_lon * LON_PAD, n_lat * MODE_PAD)
    plain, weighted = legendre_table(MM, n_rows * n_lat, n_degrees)
    split = (n_degrees, n_lat, m_local, n_lat, n_rows)
    weighted = weighted.reshape(split).transpose(1, 2, 0, 3, 4).reshape(n_lat, m_local, n_degrees, n_lat * n_rows)
    padded = np.zeros((n_lat, m_local, n_lat, 8, n_degrees))
    padded[:, :, :, :n_rows] = plain.reshape(split).transpose(1, 2, 3, 4, 0)
    padded = padded.reshape(n_lat, m_local, n_lat * 8, n_degrees)
    return tuple(t.astype(BF16) for t in (forward, inverse, weighted, padded))


def normed_parts(values):
    scale = 1.0 / values.shape[-1]
    mean = jnp.sum(values, axis=-1, keepdims=True) * scale
    center = values - mean
    spread = jnp.sum(center * center, axis=-1, keepdims=True) * scale
    return center, mean, lax.rsqrt(spread + 1e-05)


def layer_norm(values, gain):
    center, _, scale = normed_parts(values)
    return center * scale * gain


def lon_peer(me, d):
    return lax.rem(me // 2 + d // 2, 2) * 2 + lax.rem(lax.rem(me, 2) + d % 2, 2)


def spec_kernel(
    tick, n_section, plan, cutoff, lmax, mmax, *refs,
):
    if tick == 0:
        tok_hbm, prior_hbm, *refs = refs
    else:
        tok_hbm, prior_hbm, other_gains, x_next, *refs = refs
    cut_table, gains, filters, fwd, inv, leg_hbm, legt_hbm, v_out, own_out, sib_out, *refs = refs
    if tick == 0:
        x_next, *refs = refs
    (
        tok, prior, norm, ahead, x_all, spec, y_all, y_f32, f_f32, back, z_all, o_all, r_all, vbuf, nbuf, leg, legt,
        a_send, a_recv, e_send, f_recv, t_send, t_recv, b_send, b_recv, c_send, c_recv, d_send, d_recv, n_send, n_recv, loc, row_in, next_sem,
        stat, stat_in, stat_sem,
    ) = refs
    section, lat, lon = (lax.axis_index(a) for a in ("section", "lat", "lon"))
    n_lat = spec.shape[1]
    n_rows, n_cols, width = tok.shape
    n_degrees, part = filters.shape[3], filters.shape[4]
    m_local = leg.shape[0]
    half = part // 2
    sibling = lon_peer(lon, 1)
    handing = tick > 0
    first_section = section == 0

    barrier = pltpu.get_barrier_semaphore()
    greeted = 3 + n_lat - 1
    for d in (1, 2, 3):
        pl.semaphore_signal(barrier, inc=1, device_id={"lon": lon_peer(lon, d)}, device_id_type=MESH)
    if handing:
        greeted += 4
        for q in range(4):
            pl.semaphore_signal(barrier, inc=1, device_id={"section": 1 - section, "lon": q}, device_id_type=MESH)

    def greet(d, carry):
        pl.semaphore_signal(barrier, inc=1, device_id={"lat": lax.rem(lat + d, n_lat)}, device_id_type=MESH)
        return carry

    lax.fori_loop(1, n_lat, greet, 0)

    def get_tok(j):
        return pltpu.make_async_copy(tok_hbm.at[j], tok.at[j], row_in.at[0, j])

    def get_prior(j):
        return pltpu.make_async_copy(prior_hbm.at[j], prior.at[j], row_in.at[1, j])

    def get_next(h):
        return pltpu.make_async_copy(x_next.at[h], x_all.at[h], next_sem.at[h])

    def put_next(h):
        return pltpu.make_async_copy(ahead.at[h, lon], x_next.at[h, lon], next_sem.at[h])

    def over_rows(step):
        def body(j, carry):
            step(j)
            return carry

        lax.fori_loop(0, n_rows, body, 0)

    if handing:

        @pl.when(first_section)
        def _():
            over_rows(lambda j: get_prior(j).start())
            for h in (0, 1):
                get_next(h).start()
            over_rows(lambda j: get_tok(j).start())
    else:
        over_rows(lambda j: get_tok(j).start())

        @pl.when(first_section)
        def _():
            over_rows(lambda j: get_prior(j).start())
    get_leg = pltpu.make_async_copy(leg_hbm.at[lat], leg, loc.at[0])
    get_legt = pltpu.make_async_copy(legt_hbm.at[lat], legt, loc.at[1])
    get_leg.start()
    get_legt.start()

    block = plan[tick, section]
    cut = cutoff[tick - section + n_section - 1]
    l_max, m_max = lmax[section], mmax[section]
    embed = cut_table[pl.ds(cut, 1), :]
    gain_one = gains[0, block, 0:1, :]
    gain_two = gains[0, block, 1:2, :]
    pad = jnp.zeros((2, 4, n_rows, 16, half), BF16)
    ahead[:, :, :, LON_PAD - 16 :, :] = pad
    if not handing:
        norm[:, :, :, LON_PAD - 16 :, :] = pad
    f_f32[...] = jnp.zeros_like(f_f32)
    nbuf[:, LON_PAD - 16 :, :] = jnp.zeros((n_rows, 16, width), BF16)
    pl.semaphore_wait(barrier, greeted)

    def copy_a(h, j, d, sending):
        peer = lon_peer(lon, d)
        slot = lon if sending else peer
        return pltpu.make_async_remote_copy(
            src_ref=norm.at[h, peer, j] if sending else x_all.at[h, slot, j], dst_ref=x_all.at[h, slot, j], send_sem=a_send.at[h, d, j],
            recv_sem=a_recv.at[h, d, j], device_id={"lon": peer}, device_id_type=MESH)

    def copy_e(h, j, d):
        peer = lon_peer(lon, d)
        return pltpu.make_async_remote_copy(
            src_ref=ahead.at[h, peer, j], dst_ref=x_all.at[h, lon, j], send_sem=e_send.at[h, d, j],
            recv_sem=a_recv.at[h, d, j], device_id={"section": 1 - section, "lon": peer}, device_id_type=MESH)

    def copy_f(h, j, d, sending):
        peer = lon_peer(lon, d)
        slot = lon if sending else peer
        return pltpu.make_async_remote_copy(
            src_ref=ahead.at[h, peer, j], dst_ref=x_next.at[h, slot, j], send_sem=e_send.at[h, d, j],
            recv_sem=f_recv.at[h, d, j], device_id={"lon": peer}, device_id_type=MESH)

    def copy_t(d):
        quarter = pl.ds(pl.multiple_of(lon_peer(lon, d) * part, part), part)
        return pltpu.make_async_remote_copy(
            src_ref=prior.at[:, :, quarter], dst_ref=tok.at[:, :, quarter], send_sem=t_send.at[d], recv_sem=t_recv.at[d],
            device_id={"section": 1 - section}, device_id_type=MESH)

    def copy_stat():
        return pltpu.make_async_remote_copy(
            src_ref=stat, dst_ref=stat_in, send_sem=stat_sem.at[0], recv_sem=stat_sem.at[1],
            device_id={"section": 1 - section}, device_id_type=MESH)

    def split_into(dst, j, out):
        for q in range(4):
            for h in (0, 1):
                at = q * part + h * half
                dst[h, q, j, 0:n_cols, :] = out[:, at : at + half]

    def first_norm(j):
        get_tok(j).wait()
        split_into(norm, j, layer_norm(tok[j].astype(F32) + embed, gain_one).astype(BF16))
        for d in (2, 3, 1):
            copy_a(0, j, d, True).start()
        for h in (0, 1):
            x_all[h, lon, j] = norm[h, lon, j]

    def first_norm_rest(j):
        for d in (2, 3, 1):
            copy_a(1, j, d, True).start()

    if handing:

        @pl.when(first_section)
        def _():
            next_block = plan[tick, 1]
            next_embed = cut_table[pl.ds(cutoff[tick - 1 + n_section - 1], 1), :]
            next_gain = other_gains[0, next_block, 0:1, :]

            stat[...] = jnp.zeros_like(stat)
            lane = lax.broadcasted_iota(jnp.int32, (n_cols, stat.shape[1]), 1)

            def norm_ahead(j):
                get_prior(j).wait()
                raw = prior[j].astype(F32)
                center, mean, scale = normed_parts(raw + next_embed)
                out = center * scale * next_gain
                for q in range(4):
                    at = slice(q * part, (q + 1) * part)
                    mixed = jnp.where(lon == q, raw[:, at], out[:, at]).astype(BF16)
                    for h in (0, 1):
                        ahead[h, q, j, 0:n_cols, :] = mixed[:, h * half : (h + 1) * half]
                for d in range(4):
                    copy_e(0, j, d).start()
                old = stat[0:n_cols, :]
                stat[0:n_cols, :] = jnp.where(lane == 2 * j, mean, jnp.where(lane == 2 * j + 1, scale, old))

            def norm_ahead_rest(j):
                for d in range(4):
                    copy_e(1, j, d).start()

            over_rows(norm_ahead)
            copy_stat().start()
            over_rows(norm_ahead_rest)
            for d in (1, 2, 3):
                copy_t(d).start()
    else:
        over_rows(first_norm)
        over_rows(first_norm_rest)

        @pl.when(first_section)
        def _():
            next_block = plan[tick + 1, 0]
            next_embed = cut_table[pl.ds(cutoff[tick + 1 + n_section - 1], 1), :]
            next_gain = gains[0, next_block, 0:1, :]

            def norm_next(j):
                get_prior(j).wait()
                split_into(ahead, j, layer_norm(prior[j].astype(F32) + next_embed, next_gain).astype(BF16))
                for h in (0, 1):
                    for d in (2, 3, 1):
                        copy_f(h, j, d, True).start()

            over_rows(norm_next)
            for h in (0, 1):
                put_next(h).start()

    def moved(src, dst, send, recv, sending, h, d):
        peer = lax.rem(lat + d, n_lat)
        origin = lax.rem(lat - d + n_lat, n_lat)
        where = lat if sending else origin
        return pltpu.make_async_remote_copy(
            src_ref=src.at[h, peer], dst_ref=dst.at[h, where],
            send_sem=send.at[h, d], recv_sem=recv.at[h, d], device_id={"lat": peer}, device_id_type=MESH)

    def over_lat(step):
        def body(d, carry):
            step(d)
            return carry

        lax.fori_loop(1, n_lat, body, 0)

    def take_a(h, j):
        for d in (1, 2, 3):
            copy_a(h, j, d, False).wait_recv()

    def of_lon(row, h):
        out = row[:, h * half : (h + 1) * half]
        for q in (1, 2, 3):
            out = jnp.where(lon == q, row[:, q * part + h * half : q * part + (h + 1) * half], out)
        return out

    def arrived(h, j):
        if not handing:
            return x_all[h, :, j].reshape(4 * LON_PAD, half)
        shift, gain = of_lon(embed, h), of_lon(gain_one, h)
        own = x_all[h, lon, j].astype(F32)
        own = (own + shift - stat_in[:, 2 * j : 2 * j + 1]) * stat_in[:, 2 * j + 1 : 2 * j + 2] * gain
        rows_of = []
        for q in range(4):
            is_raw = jnp.logical_and(section > 0, lon == q)
            rows_of.append(jnp.where(is_raw, own, x_all[h, q, j].astype(F32)).astype(BF16))
        return jnp.concatenate(rows_of, axis=0)

    def zonal(h, first, count):
        if handing:

            @pl.when(jnp.logical_not(first_section))
            def _():
                for j in range(first, first + count):
                    copy_e(h, j, 0).wait_recv()
                    take_a(h, j)
        else:
            for j in range(first, first + count):
                take_a(h, j)

        wide = jnp.concatenate([arrived(h, j) for j in range(first, first + count)], axis=1)
        out = jnp.dot(fwd[...], wide, preferred_element_type=F32).astype(BF16)
        for i in range(count):
            spec[h, :, first + i] = out[:, i * half : (i + 1) * half].reshape(n_lat, MODE_PAD, half)

    for h in (0, 1):
        if handing:

            @pl.when(first_section)
            def _(h=h):
                get_next(h).wait()

            if h == 0:

                @pl.when(jnp.logical_not(first_section))
                def _():
                    copy_stat().wait_recv()

        for first, count in ROWS:
            zonal(h, first, count)
        if handing:
            over_lat(lambda d, h=h: moved(spec, y_all, b_send, b_recv, True, h, d).start())
    if not handing:
        for h in (0, 1):
            over_lat(lambda d, h=h: moved(spec, y_all, b_send, b_recv, True, h, d).start())

    rows = n_rows * MODE_PAD
    n_lines = n_lat * n_rows
    degree = lax.broadcasted_iota(jnp.int32, (n_degrees, half), 0)
    get_leg.wait()
    get_legt.wait()

    for h in (0, 1):

        def widen(src, value, h=h):
            at = pl.multiple_of(src * rows, 16)
            y_f32[h, pl.ds(at, rows), :] = value.reshape(rows, half).astype(F32)

        widen(lat, spec[h, lat])

        def take_b(d, h=h):
            moved(spec, y_all, b_send, b_recv, False, h, d).wait_recv()
            origin = lax.rem(lat - d + n_lat, n_lat)
            widen(origin, y_all[h, origin])

        over_lat(take_b)
        fil_re = filters[0, block, 0, :, h * half : (h + 1) * half]
        fil_im = filters[0, block, 1, :, h * half : (h + 1) * half]
        for m in range(m_local):
            pieces = [y_f32[h, pl.ds(r * m_local + m, n_lines, stride=MODE_PAD), :] for r in (0, 1)]
            column = jnp.concatenate(pieces, axis=1).astype(BF16)
            coeff = jnp.dot(leg[m], column, preferred_element_type=F32)
            co_re, co_im = coeff[:, :half], coeff[:, half:]
            order = lat * m_local + m
            keep = (degree < l_max) & (jnp.full((n_degrees, half), order, jnp.int32) < m_max)
            out_re = jnp.where(keep, co_re * fil_re - co_im * fil_im, 0.0)
            out_im = jnp.where(keep, co_re * fil_im + co_im * fil_re, 0.0)
            out = jnp.concatenate([out_re, out_im], axis=1).astype(BF16)
            lines = jnp.dot(legt[m], out, preferred_element_type=F32)
            for r in (0, 1):
                f_f32[h, pl.ds(r * m_local + m, n_lat * 8, stride=MODE_PAD), :] = lines[:, r * half : (r + 1) * half]

        def narrow(peer, h=h):
            at = pl.multiple_of(peer * (8 * MODE_PAD), 16)
            return f_f32[h, pl.ds(at, rows), :].astype(BF16).reshape(n_rows, MODE_PAD, half)

        def send_c(d, h=h):
            peer = lax.rem(lat + d, n_lat)
            back[h, peer] = narrow(peer)
            moved(back, z_all, c_send, c_recv, True, h, d).start()

        over_lat(send_c)
        z_all[h, lat] = narrow(lat)

    def copy_d(h, j, d, sending):
        peer = lon_peer(lon, d)
        slot = lon if sending else peer
        return pltpu.make_async_remote_copy(
            src_ref=o_all.at[h, peer, j], dst_ref=r_all.at[h, slot, j], send_sem=d_send.at[h, d, j],
            recv_sem=d_recv.at[h, d, j], device_id={"lon": peer}, device_id_type=MESH)

    for h in (0, 1):
        over_lat(lambda d, h=h: moved(back, z_all, c_send, c_recv, False, h, d).wait_recv())
        for first, count in ROWS:
            modes = jnp.concatenate(
                [z_all[h, :, j].reshape(n_lat * MODE_PAD, half) for j in range(first, first + count)], axis=1)
            out = jnp.dot(inv[...], modes, preferred_element_type=F32).astype(BF16)
            for i in range(count):
                j = first + i
                o_all[h, :, j] = out[:, i * half : (i + 1) * half].reshape(4, LON_PAD, half)
                for d in (2, 3, 1):
                    copy_d(h, j, d, True).start()
                r_all[h, lon, j] = o_all[h, lon, j]

    def put_v(j):
        return pltpu.make_async_copy(vbuf.at[j], v_out.at[j], loc.at[2 + j])

    def put_own(j):
        return pltpu.make_async_copy(nbuf.at[j], own_out.at[j], loc.at[2 + n_rows + j])

    def put_sib(j):
        return pltpu.make_async_remote_copy(
            src_ref=nbuf.at[j], dst_ref=sib_out.at[j], send_sem=n_send.at[j], recv_sem=n_recv.at[j],
            device_id={"lon": sibling}, device_id_type=MESH)

    if handing:

        @pl.when(jnp.logical_not(first_section))
        def _():
            for d in (1, 2, 3):
                copy_t(d).wait_recv()

            def assemble(j):
                for h in (0, 1):
                    mine = pl.ds(pl.multiple_of(lon * part + h * half, half), half)
                    tok[j, :, mine] = x_all[h, lon, j, 0:n_cols, :]

            over_rows(assemble)

        @pl.when(first_section)
        def _():
            over_rows(lambda j: get_tok(j).wait())

    def second_norm(j):
        for h in (0, 1):
            for d in (1, 2, 3):
                copy_d(h, j, d, False).wait_recv()
        spectral = jnp.concatenate(
            [r_all[h, q, j, 0:n_cols, :] for q in range(4) for h in (0, 1)], axis=1).astype(F32)
        mixed = tok[j].astype(F32) + embed + spectral
        vbuf[j] = mixed
        nbuf[j, 0:n_cols, :] = layer_norm(mixed, gain_two).astype(BF16)
        put_sib(j).start()
        put_v(j).start()
        put_own(j).start()

    over_rows(second_norm)

    def finish_a(j):
        for h in (0, 1):
            for d in (1, 2, 3):
                copy_a(h, j, d, True).wait_send()

    def finish_rows(j):
        for h in (0, 1):
            for d in (1, 2, 3):
                copy_d(h, j, d, True).wait_send()
        put_v(j).wait()
        put_own(j).wait()
        put_sib(j).wait()

    def finish_lat(d):
        for h in (0, 1):
            moved(spec, y_all, b_send, b_recv, True, h, d).wait_send()
            moved(back, z_all, c_send, c_recv, True, h, d).wait_send()

    if handing:

        def finish_handing(j):
            for h in (0, 1):
                for d in range(4):
                    copy_e(h, j, d).wait_send()

        @pl.when(first_section)
        def _():
            over_rows(finish_handing)
            copy_stat().wait_send()
            for d in (1, 2, 3):
                copy_t(d).wait_send()
    else:

        def finish_next(j):
            for h in (0, 1):
                for d in (1, 2, 3):
                    copy_f(h, j, d, True).wait_send()
                    copy_f(h, j, d, False).wait_recv()

        @pl.when(first_section)
        def _():
            over_rows(finish_next)
            for h in (0, 1):
                put_next(h).wait()

        over_rows(finish_a)
    over_lat(finish_lat)
    over_rows(finish_rows)


def spectral_part(tick, n_section, plan, cutoff, lmax, mmax, tokens, cut_table, gains, filters, tables, prior=()):
    n_rows, n_cols, width = tokens.shape
    fwd, inv, leg, legt = tables
    n_lat, m_local, n_degrees, n_lines = leg.shape
    part = filters.shape[4]
    half = part // 2
    smem = pl.BlockSpec(memory_space=pltpu.SMEM)
    vmem = pl.BlockSpec(memory_space=pltpu.VMEM)
    anys = pl.BlockSpec(memory_space=pltpu.HBM)
    dma = pltpu.SemaphoreType.DMA
    lonwise = pltpu.VMEM((2, 4, n_rows, LON_PAD, half), BF16)
    latwise = pltpu.VMEM((2, n_lat, n_rows, MODE_PAD, half), BF16)
    small = pltpu.VMEM((16, 128), BF16)
    tokens_buf = pltpu.VMEM((n_rows, n_cols, width), BF16)
    return pl.pallas_call(
        functools.partial(spec_kernel, tick, n_section),
        out_shape=(
            jax.ShapeDtypeStruct((n_rows, n_cols, width), F32),
            jax.ShapeDtypeStruct((n_rows, LON_PAD, width), BF16),
            jax.ShapeDtypeStruct((n_rows, LON_PAD, width), BF16),
        ) + (() if tick else (jax.ShapeDtypeStruct(lonwise.shape, BF16),)),
        in_specs=[smem] * 4 + [anys] * 2 + ([vmem, anys] if tick else []) + [vmem] * 5 + [anys] * 2,
        out_specs=(anys,) * (3 if tick else 4),
        scratch_shapes=[
            tokens_buf, tokens_buf, small if tick else lonwise, lonwise, lonwise, latwise, latwise,
            pltpu.VMEM((2, n_lines * MODE_PAD, half), F32),
            pltpu.VMEM((2, n_lat * 8 * MODE_PAD, half), F32),
            latwise, latwise, lonwise, lonwise,
            pltpu.VMEM((n_rows, n_cols, width), F32),
            pltpu.VMEM((n_rows, LON_PAD, width), BF16),
            pltpu.VMEM(leg.shape[1:], BF16),
            pltpu.VMEM(legt.shape[1:], BF16),
            dma((2, 4, n_rows)), dma((2, 4, n_rows)), dma((2, 4, n_rows)), dma((2, 4, n_rows)),
            dma((4,)), dma((4,)),
            dma((2, n_lat)), dma((2, n_lat)),
            dma((2, n_lat)), dma((2, n_lat)),
            dma((2, 4, n_rows)), dma((2, 4, n_rows)),
            dma((n_rows,)), dma((n_rows,)),
            dma((2 + 2 * n_rows,)), dma((2, n_rows)), dma((2,)),
            pltpu.VMEM((LON_PAD, 128), F32),
            pltpu.VMEM((LON_PAD, 128), F32),
            dma((2,)),
        ],
        compiler_params=pltpu.CompilerParams(
            collective_id=2 * tick, has_side_effects=True, vmem_limit_bytes=VMEM),
        cost_estimate=pl.CostEstimate(flops=5 * 10**10, bytes_accessed=10**7, transcendentals=0),
    )(plan, cutoff, lmax, mmax, tokens, *prior, cut_table, gains, filters, fwd, inv, leg, legt)


CHUNKS = 2
LATER = 2


def mlp_kernel(
    v_hbm, own_hbm, sib_hbm, w_hbm, out_hbm,
    x_all, wi, wo, acc, given, taken, vbuf, obuf, x_sem, w_sem, v_sem, o_sem, p_send, p_recv,
):
    lon = lax.axis_index("lon")
    sibling = lon_peer(lon, 1)
    n_rows, n_cols, width = v_hbm.shape
    ff = wi.shape[2]
    part = ff // CHUNKS
    shard = w_hbm.shape[1] // 2

    barrier = pltpu.get_barrier_semaphore()
    pl.semaphore_signal(barrier, inc=1, device_id={"lon": sibling}, device_id_type=MESH)

    get_x = [
        pltpu.make_async_copy(ref.at[pl.ds(first, count)], x_all.at[pl.ds(n_rows * k + first, count)], x_sem.at[2 * k + g])
        for k, ref in enumerate((sib_hbm, own_hbm))
        for g, (first, count) in enumerate(GROUPS)
    ]

    def get_wi(c):
        return pltpu.make_async_copy(w_hbm.at[:, pl.ds(0, shard), pl.ds(c * part, part)], wi.at[:, :, pl.ds(c * part, part)], w_sem.at[0, c])

    def get_wo(c):
        return pltpu.make_async_copy(w_hbm.at[:, pl.ds(shard, shard), pl.ds(c * part, part)], wo.at[:, :, pl.ds(c * part, part)], w_sem.at[1, c])

    get_v = pltpu.make_async_copy(v_hbm, vbuf, v_sem)
    get_x[0].start()
    for c in range(CHUNKS):
        get_wi(c).start()
        get_wo(c).start()
        if c == 0:
            get_x[1].start()
    get_x[2].start()
    get_x[3].start()
    get_v.start()
    pl.semaphore_wait(barrier, 1)

    def send(g):
        first, count = GROUPS[g]
        return pltpu.make_async_remote_copy(
            src_ref=given.at[pl.ds(first, count)], dst_ref=taken.at[pl.ds(first, count)],
            send_sem=p_send.at[g], recv_sem=p_recv.at[g], device_id={"lon": sibling}, device_id_type=MESH)

    def put(j):
        return pltpu.make_async_copy(obuf.at[j], out_hbm.at[j], o_sem.at[j])

    for tile in range(4):
        k, g = tile // 2, tile % 2
        first, count = GROUPS[g]
        size = count * LON_PAD
        get_x[tile].wait()

        x = x_all[pl.ds(n_rows * k + first, count)].reshape(size, width)
        pieces = CHUNKS if tile == 0 else LATER
        wide = ff // pieces
        for c in range(pieces):
            if tile == 0:
                get_wi(c).wait()
            at = c * wide
            before = jnp.dot(x, wi[:, :, at : at + wide].reshape(width, wide), preferred_element_type=F32)
            h = jax.nn.gelu(before).astype(BF16)
            if tile == 0:
                get_wo(c).wait()
            out = lax.dot_general(
                h, wo[:, :, at : at + wide].reshape(width, wide), (((1,), (1,)), ((), ())), preferred_element_type=F32)
            acc[0:size, :] = out if c == 0 else acc[0:size, :] + out
        total = acc[0:size, :].reshape(count, LON_PAD, width)
        if k == 0:
            given[pl.ds(first, count)] = total.astype(BF16)
            send(g).start()
        else:
            if g == 0:
                get_v.wait()
            send(g).wait_recv()
            for i in range(count):
                j = first + i
                other = taken[j, 0:n_cols, :].astype(F32)
                obuf[j] = (vbuf[j] + (total[i, 0:n_cols, :] + other)).astype(BF16)
                put(j).start()
    for j in range(n_rows):
        put(j).wait()
    for g in range(2):
        send(g).wait_send()


def mlp_part(tick, v, own, sib, weights):
    n_rows, n_cols, width = v.shape
    n_lat, shard, ff = weights.shape
    shard = shard // 2
    anys = pl.BlockSpec(memory_space=pltpu.HBM)
    dma = pltpu.SemaphoreType.DMA
    most = max(count for _, count in GROUPS)
    return pl.pallas_call(
        mlp_kernel,
        out_shape=jax.ShapeDtypeStruct((n_rows, n_cols, width), BF16),
        in_specs=[anys] * 4,
        out_specs=anys,
        scratch_shapes=[
            pltpu.VMEM((2 * n_rows, LON_PAD, width), BF16),
            pltpu.VMEM((n_lat, shard, ff), BF16),
            pltpu.VMEM((n_lat, shard, ff), BF16),
            pltpu.VMEM((most * LON_PAD, width), F32),
            pltpu.VMEM((n_rows, LON_PAD, width), BF16),
            pltpu.VMEM((n_rows, LON_PAD, width), BF16),
            pltpu.VMEM((n_rows, n_cols, width), F32),
            pltpu.VMEM((n_rows, n_cols, width), BF16),
            dma((4,)), dma((2, CHUNKS)), dma(()), dma((n_rows,)), dma((2,)), dma((2,)),
        ],
        compiler_params=pltpu.CompilerParams(
            collective_id=2 * tick + 1, has_side_effects=True, vmem_limit_bytes=VMEM),
        cost_estimate=pl.CostEstimate(flops=10**10, bytes_accessed=10**7, transcendentals=0),
    )(v, own, sib, weights)


def pick_kernel(tick, plan, w_in, w_out, out, sem):
    section = lax.axis_index("section")
    core = lax.rem(lax.axis_index("lon"), 2)
    shard, ff = w_in.shape[2], w_in.shape[3] // 2
    columns = pl.ds(pl.multiple_of(core * ff, ff), ff)
    copies = [
        pltpu.make_async_copy(ref.at[0, plan[tick, section], :, columns], out.at[pl.ds(k * shard, shard)], sem.at[k])
        for k, ref in enumerate((w_in, w_out))
    ]
    for copy in copies:
        copy.start()
    for copy in copies:
        copy.wait()


def own_weights(tick, plan, w_in, w_out):
    anys = pl.BlockSpec(memory_space=pltpu.HBM)
    out = jax.ShapeDtypeStruct((2 * w_in.shape[2], w_in.shape[3] // 2), BF16)
    return pl.pallas_call(
        functools.partial(pick_kernel, tick),
        out_shape=out,
        in_specs=[pl.BlockSpec(memory_space=pltpu.SMEM), anys, anys],
        out_specs=pl.BlockSpec(memory_space=pltpu.VMEM),
        scratch_shapes=[pltpu.SemaphoreType.DMA((2,))],
        compiler_params=pltpu.CompilerParams(vmem_limit_bytes=VMEM),
    )(plan, w_in, w_out)


def local(state, fresh, cutoff, plan, lmax, mmax, cutoff_table, norm_gains, filters, w_in, w_out):
    n_section = lax.axis_size("section")
    n_lat = lax.axis_size("lat")
    n_lon = lax.axis_size("lon")
    n_rows, n_cols, width = fresh.shape
    n_degrees = filters.shape[3]
    tables = [jnp.asarray(t) for t in spectral_tables(n_lat, n_lon, n_rows, n_cols, n_degrees)]
    weights = [lax.all_gather(own_weights(tick, plan, w_in, w_out), "lat", axis=0) for tick in (0, 1)]
    other_gains = passed_along(norm_gains, "section", -1)

    def spectral(tick, tokens, *more):
        return spectral_part(
            tick, n_section, plan, cutoff, lmax, mmax, tokens, cutoff_table, norm_gains, filters, tables, more)

    *parts, entering = spectral(0, state[0], fresh)
    first_out = mlp_part(0, *parts, weights[0])
    parts = spectral(1, fresh, first_out, other_gains, entering)
    second_out = mlp_part(1, *parts, weights[1])
    return (first_out[None], second_out[None])


def solution(mesh):
    return jax.shard_map(
        local,
        mesh=mesh,
        in_specs=(
            P("section", "lat", "lon", None),
            P("lat", "lon", None),
            P(),
            P(),
            P(),
            P(),
            P(),
            P("section", None, None, None),
            P("section", None, None, None, "lon"),
            P("section", None, "lat", None),
            P("section", None, "lat", None),
        ),
        out_specs=(P("section", "lat", "lon", None), P("section", "lat", "lon", None)),
        check_vma=False,
    )
```
